128 devices in a mesh: axial: 32 (over y, z, core), azim: 4 (over x).
Axes of the slice: x: 4, y: 4, z: 4, core: 2. Of those that a mesh axis runs over, the one named last changes fastest.
Arguments:
- residual: float32 [512, 384, 256], P('axial', 'azim'), may hold values from -6 to 6
- element_scale: float32 [3, 64, 48, 32], P(None, 'axial', 'azim'), may hold values from 0.5 to 2
- basis_fine: float32 [8, 8], replicated, may hold values from -2 to 2
- eigen_fine: float32 [8], replicated, may hold values from 0.5 to 4
- operator_fine: float32 [8, 8], replicated, may hold values from -2 to 2
- basis_mid: float32 [4, 4], replicated, may hold values from -3 to 3
- eigen_mid: float32 [4], replicated, may hold values from 0.5 to 4
- operator_mid: float32 [4, 4], replicated, may hold values from -3 to 3
- basis_low: float32 [2, 2], replicated, may hold values from -4 to 4
- eigen_low: float32 [2], replicated, may hold values from 0.5 to 4
- prolong_mid: float32 [8, 4], replicated, may hold values from -3 to 3
- prolong_low: float32 [4, 2], replicated, may hold values from -4 to 4
- vertex_route: int32 [32, 4, 768, 1], P('axial', 'azim'), may hold values from 0 to 63; in each aligned block of 768 rows (0 to 767, 768 to 1535, ..., all dimensions but the last counted through in order) at most 24 rows name the same one
- coarse_inverse: float32 [32, 4, 1536, 3072], P('axial', 'azim'), may hold values from -2 to 3
Outputs:
- correction: float32 [512, 384, 256], P('axial', 'azim')
The draws below stay inside these ranges and needn't reach their ends.
Inputs may be any that keep to these rules, and one draw needn't show every extreme that they name: `vertex_route`: among one device's 768 elements no coarse block is named more than 24 times, and one is named exactly 24 times.
All inputs are finite; a program needn't handle non-finite values.
Results may differ from the reference program's by a relative error of at most 0.0003.
Values sent between devices are 32-bit elements; how exact they have to be, the bound alone decides.
A program may use at most 192 MiB of HBM per device.

```python
import math
import jax
import jax.numpy as jnp
import numpy as np
from jax import lax

NODES_FINE = 8
NODES_MID = 4
NODES_LOW = 2
EA = 2
EZ = 12
ER = 32
NA = 64
NZ = 48
ELEMS = 768
BLOCKS = 64
CAP = 24
COARSE_ROWS = 3072
N_AXIAL = 32
N_AZIM = 4


def draw_coarse_inverse(key, part):
    key = jax.random.fold_in(key, 11)
    half_rows = COARSE_ROWS // 2
    shape = (N_AXIAL, N_AZIM, half_rows, COARSE_ROWS)
    spread = 0.7 / math.sqrt(COARSE_ROWS / 2)
    base = jax.random.normal(key, shape, jnp.float32) * spread
    lift = 1.0
    device_flat = lax.broadcasted_iota(jnp.int32, shape, 0) * N_AZIM + lax.broadcasted_iota(jnp.int32, shape, 1)
    row_index = lax.broadcasted_iota(jnp.int32, shape, 2)
    column_index = lax.broadcasted_iota(jnp.int32, shape, 3)
    diagonal = column_index == device_flat % 2 * half_rows + row_index
    return jnp.clip(base, -2.0, 2.0) + jnp.where(diagonal, lift, 0.0).astype(jnp.float32)


def level_of(rng, extent, cuts, smallest, largest):
    def one(dim, blocks):
        steps = jax.random.uniform(jax.random.fold_in(jax.random.fold_in(rng, 6), dim), (blocks,), jnp.float32, smallest / len(cuts), largest / len(cuts))
        return jnp.repeat(jnp.exp(steps), extent[dim] // blocks).reshape((-1,) + (1,) * (len(extent) - dim - 1))

    loudness = one(*cuts[0])
    for cut in cuts[1:]:
        loudness = loudness * one(*cut)
    return loudness


def deal_out(rng, own, number, rows, number_of, top, limit, lean):
    sequence = jax.random.permutation(rng, number_of)
    packed, common = portions_of(number_of, rows * top, limit, lean, True), portions_of(number_of, rows * top, limit, lean, False)
    places = jnp.arange(number_of)

    def named(tallies, turn):
        used = int((tallies > 0).sum())
        fixed = max(1, used // 4)
        passed = fixed + (places - fixed + turn * (used - fixed)) % max(1, number_of - fixed)
        return jnp.zeros((number_of,), jnp.int32).at[sequence[jnp.where(places < fixed, places, passed)]].set(jnp.asarray(tallies, jnp.int32))

    tallies = jnp.where(number % 4 == 0, named(packed, number // 4), named(common, number - number // 4 - 1))
    mixed = jax.random.permutation(jax.random.fold_in(own, 3), number_of)
    donor, receiver = mixed[0:number_of // 2 * 2:2], mixed[1:number_of // 2 * 2:2]
    room = jnp.minimum(tallies[donor] - 1, limit - tallies[receiver]) // 2
    room = jnp.where((donor == sequence[0]) | (receiver == sequence[0]) | (tallies[receiver] == 0), 0, jnp.maximum(room, 0))
    passed = jax.random.randint(jax.random.fold_in(own, 4), (number_of // 2,), 0, 1 << 20) % (room + 1)
    tallies = tallies.at[donor].add(-passed).at[receiver].add(passed)
    labels = jnp.searchsorted(jnp.cumsum(tallies), jnp.arange(rows * top), side="right").astype(jnp.int32)
    table = labels.reshape(top, rows).T
    table = table[jax.random.permutation(jax.random.fold_in(own, 1), rows)]
    turn = jax.random.randint(jax.random.fold_in(own, 2), (rows, 1), 0, top)
    return jnp.take_along_axis(table, (jnp.arange(top)[None, :] + turn) % top, axis=1)


def portions_of(number_of, total, reach, slope, full):
    loads = [(1 << 20) // math.isqrt(standing ** slope) + 1 for standing in range(1, number_of + 1)]
    largest = reach if full else min(reach, max(-(-total // number_of), total * loads[0] // sum(loads)))
    least = 1 if total - largest >= number_of - 1 else 0
    given, rest = [largest] + [least] * (number_of - 1), total - largest - least * (number_of - 1)
    while rest > 0:
        movable = [i for i in range(1, number_of) if given[i] < largest] or [i for i in range(1, number_of) if given[i] < reach]
        pool, remaining = sum([loads[i] for i in movable]), rest
        for i in movable:
            more = min(reach - given[i], max(1, remaining * loads[i] // pool), rest)
            given[i] = given[i] + more
            rest = rest - more
    return np.array(given)


def noise(key, extent, scale, limit, cuts=(), held_as=jnp.bfloat16):
    loudness = level_of(key, extent, cuts, -0.22, 0.18) if cuts else 1.0
    drawn = jax.random.normal(key, extent, jnp.float32) * scale * loudness
    return jnp.minimum(jnp.maximum(drawn, -limit), limit).astype(held_as)


def setup_inputs(seed: int = 0) -> dict:
    streams_of = jax.random.split(jax.random.key(seed), 15)
    residual = noise(streams_of[0], (NA * NODES_FINE, NZ * NODES_FINE, ER * NODES_FINE), 1.0, 6.0, ((0, 32), (1, 4)), jnp.float32)
    element_scale = jnp.clip(jnp.exp(math.log(2.0) - 1.3862944 * jax.random.uniform(streams_of[1], (3, NA, NZ, ER), jnp.float32) ** level_of(streams_of[1], (3, NA, NZ, ER), ((1, 32), (2, 4)), -0.2, 0.2)), 0.5, 2.0)
    basis_fine = noise(streams_of[2], (NODES_FINE, NODES_FINE), NODES_FINE ** -0.5, 2.0, (), jnp.float32)
    eigen_fine = jnp.clip(jnp.exp(jax.random.uniform(streams_of[3], (NODES_FINE,), jnp.float32, math.log(0.5), math.log(4.0))), 0.5, 4.0)
    operator_fine = noise(streams_of[4], (NODES_FINE, NODES_FINE), NODES_FINE ** -0.5, 2.0, (), jnp.float32)
    basis_mid = noise(streams_of[5], (NODES_MID, NODES_MID), NODES_MID ** -0.5, 3.0, (), jnp.float32)
    eigen_mid = jnp.clip(jnp.exp(jax.random.uniform(streams_of[6], (NODES_MID,), jnp.float32, math.log(0.5), math.log(4.0))), 0.5, 4.0)
    operator_mid = noise(streams_of[7], (NODES_MID, NODES_MID), NODES_MID ** -0.5, 3.0, (), jnp.float32)
    basis_low = noise(streams_of[8], (NODES_LOW, NODES_LOW), NODES_LOW ** -0.5, 4.0, (), jnp.float32)
    eigen_low = jnp.clip(jnp.exp(jax.random.uniform(streams_of[9], (NODES_LOW,), jnp.float32, math.log(0.5), math.log(4.0))), 0.5, 4.0)
    prolong_mid = noise(streams_of[10], (NODES_FINE, NODES_MID), NODES_MID ** -0.5, 3.0, (), jnp.float32)
    prolong_low = noise(streams_of[11], (NODES_MID, NODES_LOW), NODES_LOW ** -0.5, 4.0, (), jnp.float32)
    vertex_route_keys = jax.random.split(jax.random.fold_in(streams_of[12], 1), N_AXIAL * N_AZIM * ELEMS // (EA * EZ * ER))
    vertex_route_turns = jax.random.permutation(jax.random.fold_in(streams_of[12], 3), N_AXIAL * N_AZIM * ELEMS // (EA * EZ * ER))
    vertex_route = jax.vmap(lambda own, number: deal_out(jax.random.fold_in(streams_of[12], 2), own, number, EA * EZ * ER, N_AXIAL * N_AZIM // 2, 1, CAP, 2))(vertex_route_keys, vertex_route_turns).reshape((N_AXIAL, N_AZIM, ELEMS, 1))
    coarse_inverse = draw_coarse_inverse(jax.random.fold_in(streams_of[14], 71), 0)
    return dict(residual=residual, element_scale=element_scale, basis_fine=basis_fine, eigen_fine=eigen_fine, operator_fine=operator_fine, basis_mid=basis_mid, eigen_mid=eigen_mid, operator_mid=operator_mid, basis_low=basis_low, eigen_low=eigen_low, prolong_mid=prolong_mid, prolong_low=prolong_low, vertex_route=vertex_route, coarse_inverse=coarse_inverse)


HIGHEST = lax.Precision.HIGHEST


def apply_nodes(field_in, matrix, counts):
    along_count, around_count, across_count = counts
    inner = matrix.shape[1]
    outer = matrix.shape[0]
    blocked = field_in.reshape(along_count, inner, around_count, inner, across_count, inner)
    blocked = jnp.einsum('pi,aibjck->apbjck', matrix, blocked, precision=HIGHEST)
    blocked = jnp.einsum('qj,apbjck->apbqck', matrix, blocked, precision=HIGHEST)
    blocked = jnp.einsum('sk,apbqck->apbqcs', matrix, blocked, precision=HIGHEST)
    return blocked.reshape(along_count * outer, around_count * outer, across_count * outer)


def face_join(extended, axis, node_count):
    length = extended.shape[axis] - 2
    lower = lax.slice_in_dim(extended, 0, length, 1, axis)
    middle = lax.slice_in_dim(extended, 1, length + 1, 1, axis)
    upper = lax.slice_in_dim(extended, 2, length + 2, 1, axis)
    shape = [1, 1, 1]
    shape[axis] = length
    place_in = (jnp.arange(length, dtype=jnp.int32) % node_count).reshape(shape)
    return middle + jnp.where(place_in == node_count - 1, upper, 0.0) + jnp.where(place_in == 0, lower, 0.0)


def assemble_global(field_in, node_count):
    padded = jnp.pad(field_in, ((1, 1), (0, 0), (0, 0)))
    field_in = face_join(padded, 0, node_count)
    wrapped = jnp.concatenate([field_in[:, -1:], field_in, field_in[:, :1]], 1)
    field_in = face_join(wrapped, 1, node_count)
    padded = jnp.pad(field_in, ((0, 0), (0, 0), (1, 1)))
    return face_join(padded, 2, node_count)


def share_count(length, node_count, start, total, closed):
    indices = start + jnp.arange(length, dtype=jnp.int32)
    place_in = indices % node_count
    lower_face = (place_in == 0) & ((indices > 0) | closed)
    upper_face = (place_in == node_count - 1) & ((indices < total - 1) | closed)
    return 1.0 + lower_face.astype(jnp.float32) + upper_face.astype(jnp.float32)


def level_weight(shape, node_count, start, total):
    first_count = share_count(shape[0], node_count, start, total, False)
    second_count = share_count(shape[1], node_count, 0, shape[1], True)
    third_count = share_count(shape[2], node_count, 0, shape[2], False)
    return 1.0 / (first_count[:, None, None] * second_count[None, :, None] * third_count[None, None, :])


def level_scales(element_scale, eigen):
    node_count = eigen.shape[0]
    first_h = element_scale[0][:, None, :, None, :, None]
    second_h = element_scale[1][:, None, :, None, :, None]
    third_h = element_scale[2][:, None, :, None, :, None]
    total = (first_h * eigen[None, :, None, None, None, None]
             + second_h * eigen[None, None, None, :, None, None]
             + third_h * eigen[None, None, None, None, None, :])
    shape = element_scale.shape
    return total.reshape(shape[1] * node_count, shape[2] * node_count, shape[3] * node_count)


def smooth_level(rhs, basis, scales, weight, counts, assemble):
    spectral = apply_nodes(rhs, basis.T, counts) / scales
    return weight * assemble(apply_nodes(spectral, basis, counts), basis.shape[0])


def operate_level(field_in, operator, scales, counts, assemble):
    spectral = apply_nodes(field_in, operator.T, counts) * scales
    return assemble(apply_nodes(spectral, operator, counts), operator.shape[0])


def coarse_global(low_rhs, vertex_route, coarse_inverse):
    devices = N_AXIAL * N_AZIM
    half_cap = CAP // 2
    values = low_rhs[0::2, 0::2, 0::2]
    values = values.reshape(N_AXIAL, EA, N_AZIM, EZ, ER).transpose(0, 2, 1, 3, 4).reshape(devices, ELEMS)
    target = vertex_route.reshape(devices, ELEMS).astype(jnp.int32)
    member = (target[:, :, None] == jnp.arange(BLOCKS, dtype=jnp.int32)[None, None, :]).astype(jnp.int32)
    slot_rank = jnp.sum((jnp.cumsum(member, axis=1).astype(jnp.int32) - 1) * member, axis=2).astype(jnp.int32)
    source = jnp.arange(devices, dtype=jnp.int32)[:, None]
    position = (target * COARSE_ROWS + (slot_rank // half_cap) * (devices * half_cap)
                + source * half_cap + slot_rank % half_cap).astype(jnp.int32)
    vector = jnp.zeros((BLOCKS * COARSE_ROWS,), jnp.float32).at[position.reshape(-1)].set(values.reshape(-1))
    matrices = coarse_inverse.reshape(BLOCKS, COARSE_ROWS, COARSE_ROWS)
    solved = jnp.einsum('cij,cj->ci', matrices, vector.reshape(BLOCKS, COARSE_ROWS), precision=HIGHEST)
    answers = solved.reshape(-1)[position]
    answers = answers.reshape(N_AXIAL, N_AZIM, EA, EZ, ER).transpose(0, 2, 1, 3, 4).reshape(NA, NZ, ER)
    placed = jnp.zeros_like(low_rhs).at[0::2, 0::2, 0::2].set(answers)
    return assemble_global(placed, 2)


def reference(residual, element_scale, basis_fine, eigen_fine, operator_fine, basis_mid, eigen_mid, operator_mid, basis_low, eigen_low, prolong_mid, prolong_low, vertex_route, coarse_inverse):
    counts = (NA, NZ, ER)
    fine_nodes = basis_fine.shape[0]
    mid_nodes = basis_mid.shape[0]
    low_nodes = basis_low.shape[0]
    weight_fine = level_weight(residual.shape, fine_nodes, 0, NA * fine_nodes)
    scales_fine = level_scales(element_scale, eigen_fine)
    fine_first = smooth_level(residual, basis_fine, scales_fine, weight_fine, counts, assemble_global)
    fine_rest = residual - operate_level(fine_first, operator_fine, scales_fine, counts, assemble_global)
    fine_smooth = fine_first + smooth_level(fine_rest, basis_fine, scales_fine, weight_fine, counts, assemble_global)
    fine_left = residual - operate_level(fine_smooth, operator_fine, scales_fine, counts, assemble_global)
    mid_rhs = assemble_global(apply_nodes(weight_fine * fine_left, prolong_mid.T, counts), mid_nodes)
    weight_mid = level_weight(mid_rhs.shape, mid_nodes, 0, NA * mid_nodes)
    scales_mid = level_scales(element_scale, eigen_mid)
    mid_smooth = smooth_level(mid_rhs, basis_mid, scales_mid, weight_mid, counts, assemble_global)
    mid_left = mid_rhs - operate_level(mid_smooth, operator_mid, scales_mid, counts, assemble_global)
    low_rhs = assemble_global(apply_nodes(weight_mid * mid_left, prolong_low.T, counts), low_nodes)
    weight_low = level_weight(low_rhs.shape, low_nodes, 0, NA * low_nodes)
    scales_low = level_scales(element_scale, eigen_low)
    low_smooth = smooth_level(low_rhs, basis_low, scales_low, weight_low, counts, assemble_global)
    coarse_field = coarse_global(low_rhs, vertex_route, coarse_inverse)
    low_total = low_smooth + coarse_field
    mid_total = mid_smooth + apply_nodes(low_total, prolong_low, counts)
    return fine_smooth + apply_nodes(mid_total, prolong_mid, counts)
```

```python
import functools

import jax
import jax.numpy as jnp
from jax import lax
from jax.experimental import pallas as pl
from jax.experimental.pallas import tpu as pltpu
from jax.sharding import PartitionSpec as P

F32 = jnp.float32
BF = jnp.bfloat16
HIGHEST = lax.Precision.HIGHEST
MESH = pl.DeviceIdType.MESH

EZ, ER = 12, 32
HALF_CAP = 12
DIRS = ((1, 0), (-1, 0), (0, 1), (0, -1), (1, 1), (1, -1), (-1, 1), (-1, -1))


def iota(shape, dim):
    return lax.broadcasted_iota(jnp.int32, shape, dim)


def split(x):
    high = x.astype(BF)
    return high, (x - high.astype(F32)).astype(BF)


def mm(a, b):
    return jnp.dot(a, b, preferred_element_type=F32)


def mm_right(x, table):
    high, low = split(x)
    return mm(high, table[0]) + mm(high, table[1]) + mm(low, table[0])


def mm_left(table, x):
    high, low = split(x)
    return mm(table[0], high) + mm(table[1], high) + mm(table[0], low)


def stacked_right(x, table):
    high, low = split(x)
    return mm(jnp.concatenate([high, high, low], 1), table)


def stacked_left(table, x):
    high, low = split(x)
    return mm(table, jnp.concatenate([high, high, low], 0))


def picked(condition):
    return jnp.where(condition, 1.0, 0.0).astype(F32)


def quotient(x, size, count):
    if size & (size - 1) == 0:
        return x >> (size.bit_length() - 1)
    total = jnp.zeros_like(x)
    for k in range(1, count):
        total = total + jnp.where(x >= size * k, 1, 0)
    return total


def tables_of(ref):
    m, n = ref.shape
    row, lane = iota((8, 128), 0), iota((8, 128), 1)
    plain = jnp.where(lane < 8, row * 8 + lane, -1)
    turned = jnp.where(lane < 8, lane * 8 + row, -1)
    table = jnp.zeros((8, 128), F32)
    transposed = jnp.zeros((8, 128), F32)
    for i in range(m):
        for j in range(n):
            value = ref[i, j]
            table = jnp.where(plain == i * 8 + j, value, table)
            transposed = jnp.where(turned == i * 8 + j, value, transposed)
    return table, transposed


def spread_columns(table, count, length, place):
    index = place(iota((8, length), 1))
    result = jnp.zeros((8, length), F32)
    for j in range(count):
        result = jnp.where(index == j, table[:, j : j + 1], result)
    return result


def spread_rows(table, length, place):
    high = table.astype(BF).astype(F32)
    rest = table - high
    middle = rest.astype(BF).astype(F32)
    pieces = jnp.concatenate([high, middle, rest - middle], 0).astype(BF)
    index = place(iota((length, 24), 0))
    return mm(picked((iota((length, 24), 1) & 7) == index).astype(BF), pieces)


def left_table(table, m, n, group, joined=False, weighted=False, weigh_input=False):
    rows, columns = m * group * m, n * group * n

    def parts(x, nodes):
        outer = quotient(x, group * nodes, nodes)
        inner = x - outer * (group * nodes)
        block = quotient(inner, nodes, group)
        return outer, block, inner - block * nodes

    first = spread_columns(table, n, columns, lambda x: parts(x, n)[0])
    second = spread_columns(table, n, columns, lambda x: parts(x, n)[2])
    outer = spread_rows(first, rows, lambda x: parts(x, m)[0])
    inner = spread_rows(second, rows, lambda x: parts(x, m)[2])
    shape = (rows, columns)
    _, row_block, q = parts(iota(shape, 0), m)
    _, column_block, j = parts(iota(shape, 1), n)
    value = jnp.where(row_block == column_block, inner, 0.0)
    if joined:
        value = value + jnp.where(
            (q == m - 1) & (row_block + 1 == column_block), second[0:1], 0.0
        )
        value = value + jnp.where(
            (q == 0) & (row_block - 1 == column_block), second[m - 1 : m], 0.0
        )
    if weighted:
        value = jnp.where((q == 0) | (q == m - 1), 0.5 * value, value)
    if weigh_input:
        value = jnp.where((j == 0) | (j == n - 1), 0.5 * value, value)
    return outer * value


def right_table(turned, m, n, joined=False, weighted=False, weigh_input=False):
    rows, columns = ER * n, ER * m
    spread = spread_columns(turned, m, columns, lambda x: x & (m - 1))
    inner = spread_rows(spread, rows, lambda x: x & (n - 1))
    shape = (rows, columns)
    row, column = iota(shape, 0), iota(shape, 1)
    row_block, k = quotient(row, n, ER), row & (n - 1)
    column_block, s = quotient(column, m, ER), column & (m - 1)
    value = jnp.where(row_block == column_block, inner, 0.0)
    if joined:
        value = value + jnp.where(
            (s == m - 1) & (column_block + 1 == row_block), inner[:, 0:1], 0.0
        )
        value = value + jnp.where(
            (s == 0) & (column_block - 1 == row_block), inner[:, m - 1 : m], 0.0
        )
    if weighted:
        shared = ((s == 0) & (column_block > 0)) | ((s == m - 1) & (column_block < ER - 1))
        value = jnp.where(shared, 0.5 * value, value)
    if weigh_input:
        shared = ((k == 0) & (row_block > 0)) | ((k == n - 1) & (row_block < ER - 1))
        value = jnp.where(shared, 0.5 * value, value)
    return value


def put_pair(ref, index, value):
    high, low = split(value)
    ref[index, 0] = high
    ref[index, 1] = low


def put_right(ref, index, value):
    size = value.shape[0]
    high, low = split(value)
    ref[index, 0:size] = high
    ref[index, size : 2 * size] = low
    ref[index, 2 * size : 3 * size] = high


def put_left(ref, index, value):
    size = value.shape[1]
    high, low = split(value)
    ref[index, :, 0:size] = high
    ref[index, :, size : 2 * size] = low
    ref[index, :, 2 * size : 3 * size] = high


def put_scales(scale_ref, eig_ref, n, scale_out, inverse_out):
    rows, lanes = EZ * n, ER * n
    spread_z = picked(quotient(iota((rows, EZ), 0), n, EZ) == iota((rows, EZ), 1))
    spread_r = picked(iota((ER, lanes), 0) == quotient(iota((ER, lanes), 1), n, ER))
    row = iota((rows, lanes), 0) & (n - 1)
    lane = iota((rows, lanes), 1) & (n - 1)
    eig_row = jnp.zeros((rows, lanes), F32)
    eig_lane = jnp.zeros((rows, lanes), F32)
    for k in range(n):
        eig_row = jnp.where(row == k, eig_ref[k], eig_row)
        eig_lane = jnp.where(lane == k, eig_ref[k], eig_lane)
    for a in range(2):
        h = []
        for d in range(3):
            wide = jnp.dot(
                scale_ref[d, a], spread_r, precision=HIGHEST, preferred_element_type=F32
            )
            h.append(
                jnp.dot(spread_z, wide, precision=HIGHEST, preferred_element_type=F32)
            )
        flat = h[1] * eig_row + h[2] * eig_lane
        for i in range(n):
            total = h[0] * eig_ref[i] + flat
            if scale_out is not None:
                scale_out[a * n + i] = total
            inverse_out[a * n + i] = 1.0 / total


def kernel(
    res_hbm, scale_ref, route_ref, inverse_hbm,
    bf_ref, ef_ref, qf_ref, bm_ref, em_ref, qm_ref, bl_ref, el_ref, pm_ref, plow_ref,
    out_ref,
    res, first, work, scale_f, inv_f, rhs_m, smooth_m, work_m, scale_m, inv_m,
    rhs_l, smooth_l, inv_l, total_l,
    right_f, left_f, right_rf, left_rf, right_pf, left_pf,
    right_m, left_m, right_rm, left_rm, right_l, left_l, right_pp, left_pp,
    dense, target_hot, slot_hot, row_hot, place_hot, sel_hot, vector, partial,
    flat_a, send_a, recv_a, flat_b, send_b, recv_b, cs_plane, cs_row, cr_plane, cr_row,
    fs_ax, fr_ax, fs_az, fr_az, fs_dg, fr_dg,
    ms_ax, mr_ax, ms_az, mr_az, ms_dg, mr_dg,
    ls_ax, lr_ax, ls_az, lr_az, ls_dg, lr_dg,
    send_sem, recv_sem, load_sem, all_sem,
    *, n_axial, n_azim,
):
    devices = n_axial * n_azim
    me_a, me_z = lax.axis_index("axial"), lax.axis_index("azim")
    me = me_a * n_azim + me_z

    def device_of(flat):
        return (flat // n_azim, lax.rem(flat, n_azim))

    def neighbour(da, dz):
        return (lax.rem(me_a + n_axial + da, n_axial), lax.rem(me_z + n_azim + dz, n_azim))

    load_res = pltpu.make_async_copy(res_hbm, res, load_sem.at[0])
    load_res.start()
    load_dense = pltpu.make_async_copy(inverse_hbm.at[0, 0], dense, load_sem.at[1])
    load_dense.start()

    barrier = pltpu.get_barrier_semaphore()

    def greet(j, carry):
        pl.semaphore_signal(
            barrier, inc=1, device_id=device_of(lax.rem(me + j, devices)), device_id_type=MESH
        )
        return carry

    lax.fori_loop(1, devices, greet, 0)

    first_device, last_device = me_a == 0, me_a == n_axial - 1
    weight_low_end = jnp.where(first_device, 1.0, 0.5).astype(F32)
    weight_high_end = jnp.where(last_device, 1.0, 0.5).astype(F32)

    faces = {
        8: (fs_ax, fr_ax, fs_az, fr_az, fs_dg, fr_dg),
        4: (ms_ax, mr_ax, ms_az, mr_az, ms_dg, mr_dg),
        2: (ls_ax, lr_ax, ls_az, lr_az, ls_dg, lr_dg),
    }
    pending = []

    def copies_of(e, slot, n):
        s_ax, r_ax, s_az, r_az, s_dg, r_dg = faces[n]
        made = []
        for d, (da, dz) in enumerate(DIRS):
            if d < 2:
                source, target = s_ax.at[slot, d], r_ax.at[slot, d]
            elif d < 4:
                source, target = s_az.at[slot, d - 2], r_az.at[slot, d - 2]
            else:
                source, target = s_dg.at[slot, d - 4], r_dg.at[slot, d - 4]
            made.append(
                pltpu.make_async_remote_copy(
                    src_ref=source, dst_ref=target,
                    send_sem=send_sem.at[e, d], recv_sem=recv_sem.at[e, d],
                    device_id=neighbour(da, dz), device_id_type=MESH,
                )
            )
        return made

    def send_faces(e, slot, n, buf, step, weighted):
        planes, rows, _ = buf.shape
        if step is not None:
            for at in range(step, rows, step):
                both = buf[:, at - 1 : at, :] + buf[:, at : at + 1, :]
                buf[:, at - 1 : at, :] = both
                buf[:, at : at + 1, :] = both
        both = buf[n - 1] + buf[n]
        if weighted:
            both = 0.5 * both
        buf[n - 1] = both
        buf[n] = both
        s_ax, _, s_az, _, s_dg, _ = faces[n]
        s_ax[slot, 0] = buf[planes - 1]
        s_ax[slot, 1] = buf[0]
        s_dg[slot, 0] = buf[planes - 1, rows - 1 : rows]
        s_dg[slot, 1] = buf[planes - 1, 0:1]
        s_dg[slot, 2] = buf[0, rows - 1 : rows]
        s_dg[slot, 3] = buf[0, 0:1]
        for i in range(planes):
            s_az[slot, 0, i : i + 1] = buf[i, rows - 1 : rows]
            s_az[slot, 1, i : i + 1] = buf[i, 0:1]
        made = copies_of(e, slot, n)
        for copy in made:
            copy.start()
        pending.extend(made)
        return made

    def join_faces(made, slot, n, buf, weighted):
        planes, rows, _ = buf.shape
        _, r_ax, _, r_az, _, r_dg = faces[n]
        for copy in made:
            copy.wait_recv()
        for i in range(planes):
            buf[i, 0:1] = buf[i, 0:1] + r_az[slot, 0, i : i + 1]
            buf[i, rows - 1 : rows] = buf[i, rows - 1 : rows] + r_az[slot, 1, i : i + 1]
        for end, plane, device, weight in (
            (0, 0, first_device, weight_low_end),
            (1, planes - 1, last_device, weight_high_end),
        ):
            buf[plane] = buf[plane] + jnp.where(device, 0.0, r_ax[slot, end])
            buf[plane, 0:1] = buf[plane, 0:1] + jnp.where(device, 0.0, r_dg[slot, 2 * end])
            buf[plane, rows - 1 : rows] = buf[plane, rows - 1 : rows] + jnp.where(
                device, 0.0, r_dg[slot, 2 * end + 1]
            )
            if weighted:
                buf[plane] = buf[plane] * weight

    def fine_loop(body):
        def step(t, carry):
            a = t // 3
            g = lax.rem(t, 3)
            body(a, g)
            return carry

        lax.fori_loop(0, 6, step, 0)

    def cut(ref, a, g, planes=8, rows=32):
        return ref.at[
            pl.ds(pl.multiple_of(a * planes, planes), planes),
            pl.ds(pl.multiple_of(g * rows, rows), rows),
        ]

    def fine_pass(source, which, factor, result):
        def body(a, g):
            x = source(a, g).reshape(256, 256)
            y = stacked_right(x, right_f[2 * which])
            z = stacked_left(left_f[2 * which], y)
            z = z * cut(factor, a, g)[...].reshape(256, 256)
            u = stacked_right(z, right_f[2 * which + 1])
            w = stacked_left(left_f[2 * which + 1], u)
            cut(result, a, g)[...] = w.reshape(8, 32, 256)

        fine_loop(body)

    basis, basis_t = tables_of(bf_ref)
    put_right(right_f, 0, right_table(basis, 8, 8))
    put_left(left_f, 0, left_table(basis_t, 8, 8, 4))
    put_right(right_f, 1, right_table(basis_t, 8, 8, joined=True, weighted=True))
    put_left(left_f, 1, left_table(basis, 8, 8, 4, joined=True, weighted=True))
    put_scales(scale_ref, ef_ref, 8, scale_f, inv_f)

    load_res.wait()
    fine_pass(lambda a, g: cut(res, a, g)[...], 0, inv_f, first)
    pl.semaphore_wait(barrier, devices - 1)
    made = send_faces(0, 0, 8, first, 32, True)

    oper, oper_t = tables_of(qf_ref)
    put_right(right_f, 2, right_table(oper, 8, 8))
    put_left(left_f, 2, left_table(oper_t, 8, 8, 4))
    put_right(right_f, 3, right_table(oper_t, 8, 8, joined=True))
    put_left(left_f, 3, left_table(oper, 8, 8, 4, joined=True))

    join_faces(made, 0, 8, first, True)
    fine_pass(lambda a, g: cut(first, a, g)[...], 1, scale_f, work)
    made = send_faces(1, 1, 8, work, 32, False)

    put_scales(scale_ref, em_ref, 4, scale_m, inv_m)
    pm, pm_t = tables_of(pm_ref)
    put_right(right_rf, 0, right_table(pm, 4, 8, joined=True, weigh_input=True))
    put_left(left_rf, 0, left_table(pm_t, 4, 8, 4, joined=True, weigh_input=True))
    basis, basis_t = tables_of(bm_ref)
    put_pair(right_m, 0, right_table(basis, 4, 4))
    put_pair(left_m, 0, left_table(basis_t, 4, 4, EZ))
    put_pair(right_m, 1, right_table(basis_t, 4, 4, joined=True, weighted=True))
    put_pair(left_m, 1, left_table(basis, 4, 4, EZ, joined=True, weighted=True))

    join_faces(made, 1, 8, work, False)
    fine_pass(lambda a, g: cut(res, a, g)[...] - cut(work, a, g)[...], 0, inv_f, out_ref)
    made = send_faces(2, 2, 8, out_ref, 32, True)

    oper, oper_t = tables_of(qm_ref)
    put_pair(right_m, 2, right_table(oper, 4, 4))
    put_pair(left_m, 2, left_table(oper_t, 4, 4, EZ))
    put_pair(right_m, 3, right_table(oper_t, 4, 4, joined=True))
    put_pair(left_m, 3, left_table(oper, 4, 4, EZ, joined=True))
    put_scales(scale_ref, el_ref, 2, None, inv_l)

    join_faces(made, 2, 8, out_ref, True)

    def add_up(a, g):
        total = cut(first, a, g)[...] + cut(out_ref, a, g)[...]
        cut(first, a, g)[...] = total
        return total

    fine_pass(add_up, 1, scale_f, work)
    made = send_faces(3, 3, 8, work, 32, False)

    plow, plow_t = tables_of(plow_ref)
    put_pair(right_rm, 0, right_table(plow, 2, 4, joined=True, weigh_input=True))
    put_pair(left_rm, 0, left_table(plow_t, 2, 4, EZ, joined=True, weigh_input=True))
    basis, basis_t = tables_of(bl_ref)
    put_pair(right_l, 0, right_table(basis, 2, 2))
    put_pair(left_l, 0, left_table(basis_t, 2, 2, EZ))
    put_pair(right_l, 1, right_table(basis_t, 2, 2, joined=True, weighted=True))
    put_pair(left_l, 1, left_table(basis, 2, 2, EZ, joined=True, weighted=True))

    join_faces(made, 3, 8, work, False)

    def restrict(a, g):
        x = cut(res, a, g)[...] - cut(work, a, g)[...]
        low = jnp.where(a == 0, weight_low_end, 0.5)
        high = jnp.where(a == 0, 0.5, weight_high_end)
        x = jnp.concatenate([x[0:1] * low, x[1:7], x[7:8] * high], 0)
        y = stacked_right(x.reshape(256, 256), right_rf[0])
        z = stacked_left(left_rf[0], y)
        cut(rhs_m, a, g, 4, 16)[...] = z.reshape(4, 16, 128)

    fine_loop(restrict)
    made = send_faces(4, 0, 4, rhs_m, 16, False)

    route = route_ref[...]
    hot = picked(iota((64, 768), 0) == route)
    target_hot[...] = hot.astype(BF)
    earlier = picked(iota((768, 768), 0) < iota((768, 768), 1)).astype(BF)
    rank = jnp.sum(mm(target_hot[...], earlier) * hot, axis=0, keepdims=True)
    slot_hot[...] = picked(iota((128, 768), 0).astype(F32) == rank)
    half = jnp.where(rank >= HALF_CAP, 1.0, 0.0)
    owner = 2.0 * route.astype(F32) + half
    row_hot[...] = picked(iota((128, 768), 0).astype(F32) == owner).astype(BF)
    place_hot[...] = picked(iota((16, 768), 0).astype(F32) == rank - HALF_CAP * half)

    join_faces(made, 0, 4, rhs_m, False)

    def small_pass(x, n, right, left, which, factor):
        planes, rows, lanes = x.shape
        for side in range(2):
            y = mm_right(x.reshape(planes * rows, lanes), right.at[2 * which + side])
            y = y.reshape(2, n * rows, lanes)
            z = [mm_left(left.at[2 * which + side], y[a]) for a in range(2)]
            x = jnp.concatenate([v.reshape(n, rows, lanes) for v in z], 0)
            if side == 0:
                x = x * factor[...]
        return x

    smooth_m[...] = small_pass(rhs_m[...], 4, right_m, left_m, 0, inv_m)
    made = send_faces(5, 1, 4, smooth_m, None, True)
    put_right(right_pf, 0, right_table(pm_t, 8, 4))
    put_pair(left_pf, 0, left_table(pm, 8, 4, 4))
    join_faces(made, 1, 4, smooth_m, True)

    work_m[...] = small_pass(smooth_m[...], 4, right_m, left_m, 1, scale_m)
    made = send_faces(6, 2, 4, work_m, None, False)
    both = jnp.zeros((8, 128), F32)
    both_t = jnp.zeros((8, 128), F32)
    for k in range(4):
        both = both + pm[:, k : k + 1] * plow[k : k + 1, :]
        both_t = both_t + plow_t[:, k : k + 1] * pm_t[k : k + 1, :]
    put_pair(right_pp, 0, right_table(both_t, 8, 2))
    put_pair(left_pp, 0, left_table(both, 8, 2, 4))
    join_faces(made, 2, 4, work_m, False)

    x = rhs_m[...] - work_m[...]
    x = jnp.concatenate(
        [x[0:1] * weight_low_end, x[1:3], x[3:5] * 0.5, x[5:7], x[7:8] * weight_high_end], 0
    )
    y = mm_right(x.reshape(384, 128), right_rm.at[0]).reshape(2, 192, 64)
    for a in range(2):
        rhs_l[2 * a : 2 * a + 2] = mm_left(left_rm.at[0], y[a]).reshape(2, 24, 64)
    made = send_faces(7, 0, 2, rhs_l, None, False)

    slot = iota((128, 3072), 0)
    lane = iota((1, 3072), 1)
    half_lane = jnp.where(lane >= 1536, 1, 0)
    rest = lane - 1536 * half_lane
    source = jnp.floor((rest.astype(F32) + 0.5) * (1.0 / HALF_CAP)).astype(jnp.int32)
    wanted = half_lane * HALF_CAP + rest - source * HALF_CAP
    sel_hot[...] = picked(slot == wanted).astype(BF)
    join_faces(made, 0, 2, rhs_l, False)

    values = []
    lane = iota((24, 384), 1)
    mine = iota((24, 384), 0) == 2 * (lane >> 5)
    pick_r = picked(iota((64, 384), 0) == 2 * (iota((64, 384), 1) & 31))
    for a in range(2):
        wide = jnp.dot(rhs_l[2 * a], pick_r, precision=HIGHEST, preferred_element_type=F32)
        values.append(jnp.sum(jnp.where(mine, wide, 0.0), axis=0, keepdims=True))
    values = jnp.concatenate(values, 1)
    high, low = split(slot_hot[...] * values)
    nt = (((1,), (1,)), ((), ()))
    flat_a[...] = lax.dot_general(
        target_hot[...], high, nt, preferred_element_type=F32
    ) + lax.dot_general(target_hot[...], low, nt, preferred_element_type=F32)
    for t in range(64):
        send_a[t] = flat_a[t : t + 1]

    def spread_out(source_of, target, sem, row_of):
        def start(j, carry):
            other = lax.rem(me + j, devices)
            pltpu.make_async_remote_copy(
                src_ref=source_of.at[row_of(other)], dst_ref=target.at[me],
                send_sem=all_sem.at[sem], recv_sem=all_sem.at[sem + 1],
                device_id=device_of(other), device_id_type=MESH,
            ).start()
            return carry

        lax.fori_loop(1, devices, start, 0)
        target[me] = source_of[row_of(me)]

    def wait_all(target, sem):
        some = target.at[pl.ds(0, devices - 1)]
        pltpu.make_async_copy(some, some, all_sem.at[sem]).wait()

    spread_out(send_a, recv_a, 0, lambda other: other // 2)

    smooth_l[...] = small_pass(rhs_l[...], 2, right_l, left_l, 0, inv_l)
    made = send_faces(8, 1, 2, smooth_l, None, True)

    def prolong(a, g):
        x = cut(smooth_m, a, g, 4, 16)[...].reshape(64, 128)
        y = stacked_right(x, right_pf[0])
        z = mm_left(left_pf.at[0], y)
        cut(out_ref, a, g)[...] = cut(first, a, g)[...] + z.reshape(8, 32, 256)

    fine_loop(prolong)
    join_faces(made, 1, 2, smooth_l, True)

    wait_all(recv_a, 1)
    for d in range(devices):
        flat_b[d : d + 1] = recv_a[d]
    high, low = split(flat_b[...])
    wide = mm(high, sel_hot[...]) + mm(low, sel_hot[...])
    wide = jnp.where(iota((128, 3072), 0) == source, wide, 0.0)
    vector[...] = jnp.broadcast_to(jnp.sum(wide, axis=0, keepdims=True), (8, 3072))
    load_dense.wait()

    def rows_of(r, carry):
        base = pl.multiple_of(r * 32, 32)
        sums = [None] * 4
        for c in range(24):
            v = vector[:, c * 128 : (c + 1) * 128]
            for k in range(4):
                term = dense[pl.ds(base + 8 * k, 8), c * 128 : (c + 1) * 128] * v
                sums[k] = term if sums[k] is None else sums[k] + term
        for k in range(4):
            partial[pl.ds(base + 8 * k, 8), :] = sums[k]
        return carry

    lax.fori_loop(0, 48, rows_of, 0)
    high, low = split(partial[...])
    ones = jnp.ones((128, 128), BF)
    sums = mm(high, ones) + mm(low, ones)
    row = iota((1536, 128), 0)
    group = jnp.floor((row.astype(F32) + 0.5) * (1.0 / HALF_CAP)).astype(jnp.int32)
    sums = jnp.where(iota((1536, 128), 1) == row - group * HALF_CAP, sums, 0.0)
    high, low = split(sums)
    lane = iota((1, 1536), 1)
    group = jnp.floor((lane.astype(F32) + 0.5) * (1.0 / HALF_CAP)).astype(jnp.int32)
    gather = picked(iota((128, 1536), 0) == group).astype(BF)
    flat_b[...] = mm(gather, high) + mm(gather, low)
    for d in range(devices):
        send_b[d] = flat_b[d : d + 1]
    spread_out(send_b, recv_b, 2, lambda other: other)
    wait_all(recv_b, 3)
    for d in range(devices):
        flat_b[d : d + 1] = recv_b[d]

    turned = jnp.transpose(flat_b[...])[0:16]
    high, low = split(turned)
    answers = mm(high, row_hot[...]) + mm(low, row_hot[...])
    answers = jnp.sum(answers * place_hot[...], axis=0, keepdims=True)
    row = iota((24, 384), 0)
    belongs = (iota((24, 384), 1) >> 5) == ((row + 1) >> 1)
    to_lanes = picked(
        (iota((384, 64), 0) & 31) == ((iota((384, 64), 1) + 1) >> 1)
    ).astype(BF)
    grids = []
    for a in range(2):
        high, low = split(jnp.where(belongs, answers[:, a * 384 : (a + 1) * 384], 0.0))
        grids.append(mm(high, to_lanes) + mm(low, to_lanes))
    cs_plane[...] = grids[0]
    cs_row[0] = grids[0][0:1]
    cs_row[1] = grids[1][0:1]
    made = []
    for k, (source, target, da, dz) in enumerate((
        (cs_plane, cr_plane, -1, 0),
        (cs_row, cr_row.at[pl.ds(0, 2)], 0, -1),
        (cs_row.at[0], cr_row.at[2], -1, -1),
    )):
        copy = pltpu.make_async_remote_copy(
            src_ref=source, dst_ref=target,
            send_sem=send_sem.at[9, k], recv_sem=recv_sem.at[9, k],
            device_id=neighbour(da, dz), device_id_type=MESH,
        )
        copy.start()
        made.append(copy)
    pending.extend(made)
    for copy in made:
        copy.wait_recv()
    last_row = iota((24, 64), 0) == 23
    lower = jnp.where(last_row, cr_row[0], grids[0])
    upper = jnp.where(last_row, cr_row[1], grids[1])
    beyond = jnp.where(last_device, 0.0, jnp.where(last_row, cr_row[2], cr_plane[...]))
    total_l[0] = smooth_l[0] + lower
    total_l[1] = smooth_l[1] + upper
    total_l[2] = smooth_l[2] + upper
    total_l[3] = smooth_l[3] + beyond

    wide = mm_right(total_l[...].reshape(96, 64), right_pp.at[0]).reshape(4, 24, 256)
    for a in range(2):
        for g in range(3):
            x = wide[2 * a : 2 * a + 2, 8 * g : 8 * g + 8].reshape(16, 256)
            z = mm_left(left_pp.at[0], x).reshape(8, 32, 256)
            out_ref[8 * a : 8 * a + 8, 32 * g : 32 * g + 32] += z

    for copy in pending:
        copy.wait_send()
    wait_all(recv_a, 0)
    wait_all(recv_b, 2)


def on_device(
    residual, element_scale, basis_fine, eigen_fine, operator_fine, basis_mid, eigen_mid,
    operator_mid, basis_low, eigen_low, prolong_mid, prolong_low, vertex_route, coarse_inverse,
):
    devices = lax.axis_size("axial") * lax.axis_size("azim")

    def vm(*shape, dtype=F32):
        return pltpu.VMEM(shape, dtype)

    def face_buffers(count, planes, rows, lanes):
        return [
            vm(count, 2, rows, lanes), vm(count, 2, rows, lanes),
            vm(count, 2, planes, lanes), vm(count, 2, planes, lanes),
            vm(count, 4, 1, lanes), vm(count, 4, 1, lanes),
        ]

    fine, mid, low = (16, 96, 256), (8, 48, 128), (4, 24, 64)
    scratch = [
        vm(*fine), vm(*fine), vm(*fine), vm(*fine), vm(*fine),
        vm(*mid), vm(*mid), vm(*mid), vm(*mid), vm(*mid),
        vm(*low), vm(*low), vm(*low), vm(*low),
        vm(4, 768, 256, dtype=BF), vm(4, 256, 768, dtype=BF),
        vm(1, 768, 128, dtype=BF), vm(1, 64, 768, dtype=BF),
        vm(1, 384, 256, dtype=BF), vm(1, 2, 256, 64, dtype=BF),
        vm(4, 2, 128, 128, dtype=BF), vm(4, 2, 192, 192, dtype=BF),
        vm(1, 2, 128, 64, dtype=BF), vm(1, 2, 48, 192, dtype=BF),
        vm(2, 2, 64, 64, dtype=BF), vm(2, 2, 48, 48, dtype=BF),
        vm(1, 2, 64, 256, dtype=BF), vm(1, 2, 256, 16, dtype=BF),
        vm(1536, 3072), vm(64, 768, dtype=BF), vm(128, 768), vm(128, 768, dtype=BF),
        vm(16, 768), vm(128, 3072, dtype=BF), vm(8, 3072), vm(1536, 128),
        vm(64, 128), vm(64, 1, 128), vm(devices, 1, 128),
        vm(devices, 128), vm(devices, 1, 128), vm(devices, 1, 128),
        vm(24, 64), vm(2, 1, 64), vm(24, 64), vm(3, 1, 64),
        *face_buffers(4, *fine), *face_buffers(3, *mid), *face_buffers(2, *low),
        pltpu.SemaphoreType.DMA((10, 8)), pltpu.SemaphoreType.DMA((10, 8)),
        pltpu.SemaphoreType.DMA((2,)), pltpu.SemaphoreType.DMA((4,)),
    ]
    in_vmem = pl.BlockSpec(memory_space=pltpu.VMEM)
    in_smem = pl.BlockSpec(memory_space=pltpu.SMEM)
    anywhere = pl.BlockSpec(memory_space=pl.ANY)
    call = pl.pallas_call(
        functools.partial(
            kernel, n_axial=lax.axis_size("axial"), n_azim=lax.axis_size("azim")
        ),
        out_shape=jax.ShapeDtypeStruct(residual.shape, F32),
        in_specs=[anywhere, in_vmem, in_vmem, anywhere] + [in_smem] * 10,
        out_specs=in_vmem,
        scratch_shapes=scratch,
        compiler_params=pltpu.CompilerParams(
            collective_id=0, has_side_effects=True, vmem_limit_bytes=58 * 1024 * 1024
        ),
        cost_estimate=pl.CostEstimate(
            flops=12_000_000_000, bytes_accessed=24_000_000, transcendentals=0
        ),
    )
    return call(
        residual, element_scale, vertex_route.reshape(1, -1), coarse_inverse,
        basis_fine, eigen_fine, operator_fine, basis_mid, eigen_mid, operator_mid,
        basis_low, eigen_low, prolong_mid, prolong_low,
    )


def solution(mesh):
    return jax.shard_map(
        on_device,
        mesh=mesh,
        in_specs=(
            P("axial", "azim", None),
            P(None, "axial", "azim", None),
            P(), P(), P(), P(), P(), P(), P(), P(), P(), P(),
            P("axial", "azim", None, None),
            P("axial", "azim", None, None),
        ),
        out_specs=P("axial", "azim", None),
        check_vma=False,
    )
```

```python
import functools

import jax
import jax.numpy as jnp
from jax import lax
from jax.experimental import pallas as pl
from jax.experimental.pallas import tpu as pltpu
from jax.sharding import PartitionSpec as P

F32 = jnp.float32
BF = jnp.bfloat16
HIGHEST = lax.Precision.HIGHEST
MESH = pl.DeviceIdType.MESH

EZ, ER = 12, 32
HALF_CAP = 12
DIRS = ((1, 0), (-1, 0), (0, 1), (0, -1), (1, 1), (1, -1), (-1, 1), (-1, -1))


def iota(shape, dim):
    return lax.broadcasted_iota(jnp.int32, shape, dim)


def split(x):
    high = x.astype(BF)
    return high, (x - high.astype(F32)).astype(BF)


def mm(a, b):
    return jnp.dot(a, b, preferred_element_type=F32)


def mm_right(x, table):
    high, low = split(x)
    return mm(high, table[0]) + mm(high, table[1]) + mm(low, table[0])


def mm_left(table, x):
    high, low = split(x)
    return mm(table[0], high) + mm(table[1], high) + mm(table[0], low)


def wide_right(x, table):
    high, low = split(x)
    both = mm(jnp.concatenate([high, low], 1), table)
    size = table.shape[1] // 2
    return both[:, :size] + both[:, size:]


def wide_left(table, blocks):
    high, low = split(jnp.concatenate(blocks, 1))
    both = mm(table, jnp.concatenate([high, low], 0))
    size = table.shape[0] // 2
    both = both[:size] + both[size:]
    lanes = blocks[0].shape[1]
    return [both[:, k * lanes : (k + 1) * lanes] for k in range(len(blocks))]


def thrice_left(table, blocks):
    high, low = split(jnp.concatenate(blocks, 1))
    both = mm(table, jnp.concatenate([high, high, low], 0))
    lanes = blocks[0].shape[1]
    return [both[:, k * lanes : (k + 1) * lanes] for k in range(len(blocks))]


def cut_rows(x, n, rows):
    planes, length, lanes = x.shape
    return [
        x[a * n : a * n + n, r : r + rows].reshape(n * rows, lanes)
        for a in range(planes // n)
        for r in range(0, length, rows)
    ]


def paste_rows(blocks, n):
    rows, lanes = blocks[0].shape[0] // n, blocks[0].shape[1]
    half = len(blocks) // 2
    blocks = [b.reshape(n, rows, lanes) for b in blocks]
    return jnp.concatenate(
        [jnp.concatenate(blocks[:half], 1), jnp.concatenate(blocks[half:], 1)], 0
    )


def picked(condition):
    return jnp.where(condition, 1.0, 0.0).astype(F32)


def quotient(x, size, count):
    if size & (size - 1) == 0:
        return x >> (size.bit_length() - 1)
    total = jnp.zeros_like(x)
    for k in range(1, count):
        total = total + jnp.where(x >= size * k, 1, 0)
    return total


def tables_of(ref, turned_in=False):
    n, m = ref.shape if turned_in else ref.shape[::-1]
    row, lane = iota((8, 128), 0), iota((8, 128), 1)
    plain = jnp.where(lane < 8, row * 8 + lane, -1)
    turned = jnp.where(lane < 8, lane * 8 + row, -1)
    table = jnp.zeros((8, 128), F32)
    transposed = jnp.zeros((8, 128), F32)
    for i in range(m):
        for j in range(n):
            value = ref[j, i] if turned_in else ref[i, j]
            table = jnp.where(plain == i * 8 + j, value, table)
            transposed = jnp.where(turned == i * 8 + j, value, transposed)
    return table, transposed


def spread_columns(table, count, length, place):
    index = place(iota((8, length), 1))
    result = jnp.zeros((8, length), F32)
    for j in range(count):
        result = jnp.where(index == j, table[:, j : j + 1], result)
    return result


def spread_rows(table, length, place):
    high = table.astype(BF).astype(F32)
    rest = table - high
    middle = rest.astype(BF).astype(F32)
    pieces = jnp.concatenate([high, middle, rest - middle], 0).astype(BF)
    index = place(iota((length, 24), 0))
    return mm(picked((iota((length, 24), 1) & 7) == index).astype(BF), pieces)


def left_table(table, m, n, group, joined=False, weighted=False, weigh_input=False, copies=1):
    rows, columns = m * group * m, n * group * n

    def once(x):
        return x if copies == 1 else x - columns * quotient(x, columns, copies)

    def parts(x, nodes):
        outer = quotient(x, group * nodes, nodes)
        inner = x - outer * (group * nodes)
        block = quotient(inner, nodes, group)
        return outer, block, inner - block * nodes

    first = spread_columns(table, n, copies * columns, lambda x: parts(once(x), n)[0])
    second = spread_columns(table, n, copies * columns, lambda x: parts(once(x), n)[2])
    outer = spread_rows(first, rows, lambda x: parts(x, m)[0])
    inner = spread_rows(second, rows, lambda x: parts(x, m)[2])
    shape = (rows, copies * columns)
    _, row_block, q = parts(iota(shape, 0), m)
    _, column_block, j = parts(once(iota(shape, 1)), n)
    value = jnp.where(row_block == column_block, inner, 0.0)
    if joined:
        value = value + jnp.where(
            (q == m - 1) & (row_block + 1 == column_block), second[0:1], 0.0
        )
        value = value + jnp.where(
            (q == 0) & (row_block - 1 == column_block), second[m - 1 : m], 0.0
        )
    if weighted:
        value = jnp.where((q == 0) | (q == m - 1), 0.5 * value, value)
    if weigh_input:
        value = jnp.where((j == 0) | (j == n - 1), 0.5 * value, value)
    return outer * value


def right_table(
    turned, m, n, count=ER, joined=False, weighted=False, weigh_input=False,
    first=True, last=True, copies=1,
):
    rows, columns = count * n, count * m
    spread = spread_columns(turned, m, copies * columns, lambda x: x & (m - 1))
    inner = spread_rows(spread, rows, lambda x: x & (n - 1))
    shape = (rows, copies * columns)
    row, column = iota(shape, 0), iota(shape, 1) & (columns - 1)
    row_block, k = quotient(row, n, count), row & (n - 1)
    column_block, s = quotient(column, m, count), column & (m - 1)
    value = jnp.where(row_block == column_block, inner, 0.0)
    if joined:
        value = value + jnp.where(
            (s == m - 1) & (column_block + 1 == row_block), inner[:, 0:1], 0.0
        )
        value = value + jnp.where(
            (s == 0) & (column_block - 1 == row_block), inner[:, m - 1 : m], 0.0
        )

    def halved(place, block, nodes, value):
        low, high = place == 0, place == nodes - 1
        if first:
            low = low & (block > 0)
        if last:
            high = high & (block < count - 1)
        return jnp.where(low | high, 0.5 * value, value)

    if weighted:
        value = halved(s, column_block, m, value)
    if weigh_input:
        value = halved(k, row_block, n, value)
    return value


def put_pair(ref, index, value):
    high, low = split(value)
    ref[index, 0] = high
    ref[index, 1] = low


def put_right(ref, index, value):
    rows, columns = value.shape
    high, low = split(value)
    for k in range(2):
        ref[index, k * rows : (k + 1) * rows, 0:columns] = high
        ref[index, k * rows : (k + 1) * rows, columns : 2 * columns] = low


def put_left(ref, index, value):
    rows, columns = value.shape
    high, low = split(value)
    for k in range(2):
        ref[index, 0:rows, k * columns : (k + 1) * columns] = high
        ref[index, rows : 2 * rows, k * columns : (k + 1) * columns] = low


def put_left_twice(ref, index, value):
    rows = value.shape[0]
    high, low = split(value)
    ref[index, 0:rows] = high
    ref[index, rows : 2 * rows] = low


def put_left_thrice(ref, index, value):
    columns = value.shape[1] // 3
    high, low = split(value)
    lane = iota(value.shape, 1)
    middle = (lane >= columns) & (lane < 2 * columns)
    ref[index] = jnp.where(middle, low.astype(F32), high.astype(F32)).astype(BF)


def put_scales(scale_ref, eig_ref, n, scale_out, inverse_out):
    rows, lanes = EZ * n, ER * n
    spread_z = picked(quotient(iota((rows, EZ), 0), n, EZ) == iota((rows, EZ), 1))
    spread_r = picked(iota((ER, lanes), 0) == quotient(iota((ER, lanes), 1), n, ER))
    row = iota((rows, lanes), 0) & (n - 1)
    lane = iota((rows, lanes), 1) & (n - 1)
    eig_row = jnp.zeros((rows, lanes), F32)
    eig_lane = jnp.zeros((rows, lanes), F32)
    for k in range(n):
        eig_row = jnp.where(row == k, eig_ref[k], eig_row)
        eig_lane = jnp.where(lane == k, eig_ref[k], eig_lane)
    for a in range(2):
        h = []
        for d in range(3):
            wide = jnp.dot(
                scale_ref[d, :, a], spread_r, precision=HIGHEST, preferred_element_type=F32
            )
            h.append(
                jnp.dot(spread_z, wide, precision=HIGHEST, preferred_element_type=F32)
            )
        flat = h[1] * eig_row + h[2] * eig_lane
        for i in range(n):
            total = h[0] * eig_ref[i] + flat
            if scale_out is not None:
                scale_out[a * n + i] = total
            inverse_out[a * n + i] = 1.0 / total


def kernel(
    res_hbm, scale_ref, route_ref, inverse_hbm,
    bf_ref, ef_ref, qf_ref, bm_ref, em_ref, qm_ref, bl_ref, el_ref, pm_ref, plow_ref,
    out_ref,
    res, first, second, work, scale_f, inv_f, rhs_m, smooth_m, work_m, scale_m, inv_m,
    rhs_l, smooth_l, inv_l, total_l,
    right_f, left_f, right_rf, left_rf, right_pf, left_pf,
    right_m, left_m, right_rm, left_rm, right_l, left_l, right_pp, left_pp,
    dense, target_hot, slot_hot, row_hot, place_hot, sel_hot, vector, partial,
    flat_a, send_a, stage_a, recv_a, flat_b, send_b, stage_b, recv_b, cs_plane, cs_row, cr_plane, cr_row,
    fs_ax, fr_ax, fs_az, fr_az, fs_dg, fr_dg,
    ms_ax, mr_ax, ms_az, mr_az, ms_dg, mr_dg,
    ls_ax, lr_ax, ls_az, lr_az, ls_dg, lr_dg,
    send_sem, recv_sem, load_sem, all_sem,
    *, n_axial, n_azim,
):
    devices = n_axial * n_azim
    me_a, me_z = lax.axis_index("axial"), lax.axis_index("azim")

    def neighbour(da, dz):
        return (lax.rem(me_a + n_axial + da, n_axial), lax.rem(me_z + n_azim + dz, n_azim))

    load_res = pltpu.make_async_copy(res_hbm, res, load_sem.at[0])
    load_res.start()
    load_dense = pltpu.make_async_copy(inverse_hbm.at[0, 0], dense, load_sem.at[1])
    load_dense.start()

    barrier = pltpu.get_barrier_semaphore()

    def greet(device):
        pl.semaphore_signal(barrier, inc=1, device_id=device, device_id_type=MESH)

    def along(j):
        return (lax.rem(me_a + j, n_axial), me_z)

    def around(j):
        return (me_a, lax.rem(me_z + j, n_azim))

    def greet_along(j, carry):
        greet(along(j))
        return carry

    for da, dz in DIRS[4:]:
        greet(neighbour(da, dz))
    for j in range(1, n_azim):
        greet(around(j))
    lax.fori_loop(1, n_axial, greet_along, 0)
    greeted = 4 + n_azim - 1 + n_axial - 1

    first_device, last_device = me_a == 0, me_a == n_axial - 1
    weight_low_end = jnp.where(first_device, 1.0, 0.5).astype(F32)
    weight_high_end = jnp.where(last_device, 1.0, 0.5).astype(F32)

    faces = {
        8: (fs_ax, fr_ax, fs_az, fr_az, fs_dg, fr_dg),
        4: (ms_ax, mr_ax, ms_az, mr_az, ms_dg, mr_dg),
        2: (ls_ax, lr_ax, ls_az, lr_az, ls_dg, lr_dg),
    }
    pending = []

    def copies_of(e, slot, n):
        s_ax, r_ax, s_az, r_az, s_dg, r_dg = faces[n]
        made = []
        for d, (da, dz) in enumerate(DIRS):
            if d < 2:
                source, target = s_ax.at[slot, d], r_ax.at[slot, d]
            elif d < 4:
                source, target = s_az.at[slot, d - 2], r_az.at[slot, d - 2]
            else:
                source, target = s_dg.at[slot, d - 4], r_dg.at[slot, d - 4]
            made.append(
                pltpu.make_async_remote_copy(
                    src_ref=source, dst_ref=target,
                    send_sem=send_sem.at[e, d], recv_sem=recv_sem.at[e, d],
                    device_id=neighbour(da, dz), device_id_type=MESH,
                )
            )
        return made

    def send_faces(e, slot, n, buf, step, weighted):
        planes, rows, _ = buf.shape
        if step is not None:
            for at in range(step, rows, step):
                both = buf[:, at - 1 : at, :] + buf[:, at : at + 1, :]
                buf[:, at - 1 : at, :] = both
                buf[:, at : at + 1, :] = both
        both = buf[n - 1] + buf[n]
        if weighted:
            both = 0.5 * both
        buf[n - 1] = both
        buf[n] = both
        s_ax, _, s_az, _, s_dg, _ = faces[n]
        s_ax[slot, 0] = buf[planes - 1]
        s_ax[slot, 1] = buf[0]
        s_dg[slot, 0] = buf[planes - 1, rows - 1 : rows]
        s_dg[slot, 1] = buf[planes - 1, 0:1]
        s_dg[slot, 2] = buf[0, rows - 1 : rows]
        s_dg[slot, 3] = buf[0, 0:1]
        for i in range(planes):
            s_az[slot, 0, i : i + 1] = buf[i, rows - 1 : rows]
            s_az[slot, 1, i : i + 1] = buf[i, 0:1]
        made = copies_of(e, slot, n)
        for copy in made:
            copy.start()
        pending.extend(made)
        return made

    def join_faces(made, slot, n, buf, weighted):
        planes, rows, _ = buf.shape
        _, r_ax, _, r_az, _, r_dg = faces[n]
        for copy in made:
            copy.wait_recv()
        for i in range(planes):
            buf[i, 0:1] = buf[i, 0:1] + r_az[slot, 0, i : i + 1]
            buf[i, rows - 1 : rows] = buf[i, rows - 1 : rows] + r_az[slot, 1, i : i + 1]
        for end, plane, device, weight in (
            (0, 0, first_device, weight_low_end),
            (1, planes - 1, last_device, weight_high_end),
        ):
            buf[plane] = buf[plane] + jnp.where(device, 0.0, r_ax[slot, end])
            buf[plane, 0:1] = buf[plane, 0:1] + jnp.where(device, 0.0, r_dg[slot, 2 * end])
            buf[plane, rows - 1 : rows] = buf[plane, rows - 1 : rows] + jnp.where(
                device, 0.0, r_dg[slot, 2 * end + 1]
            )
            if weighted:
                buf[plane] = buf[plane] * weight

    def fine_right(x, which, joined):
        planes, rows, lanes = x.shape
        x = x.reshape(planes * rows, lanes)
        left = wide_right(x[:, :128], right_f[2 * which])
        right = wide_right(x[:, 128:], right_f[2 * which + 1])
        if joined:
            lane = iota(left.shape, 1)
            left, right = (
                left + jnp.where(lane == 127, pltpu.roll(right, 127, 1), 0.0),
                right + jnp.where(lane == 0, pltpu.roll(left, 1, 1), 0.0),
            )
        return jnp.concatenate([left, right], 1).reshape(planes, rows, lanes)

    def fine_left(x, which):
        half = 6
        blocks = cut_rows(x, 8, 16)
        table = left_f[which]
        return paste_rows(wide_left(table, blocks[:half]) + wide_left(table, blocks[half:]), 8)

    def fine_pass(x, which, factor, result):
        z = fine_left(fine_right(x, 2 * which, False), 2 * which)
        z = z * factor[...]
        result[...] = fine_left(fine_right(z, 2 * which + 1, True), 2 * which + 1)

    basis, basis_t = tables_of(bf_ref)

    def put_fine(at, table, turned, weighted):
        value = right_table(table, 8, 8, 16)
        put_right(right_f, 4 * at, value)
        put_right(right_f, 4 * at + 1, value)
        put_left(left_f, 2 * at, left_table(turned, 8, 8, 2))
        for end in range(2):
            value = right_table(
                turned, 8, 8, 16, joined=True, weighted=weighted, first=end == 0, last=end == 1
            )
            put_right(right_f, 4 * at + 2 + end, value)
        put_left(left_f, 2 * at + 1, left_table(table, 8, 8, 2, joined=True, weighted=weighted))

    put_fine(0, basis, basis_t, True)
    put_scales(scale_ref, ef_ref, 8, scale_f, inv_f)

    load_res.wait()
    fine_pass(res[...], 0, inv_f, first)
    pl.semaphore_wait(barrier, greeted)
    made = send_faces(0, 0, 8, first, 16, True)

    oper, oper_t = tables_of(qf_ref)
    put_fine(1, oper, oper_t, False)

    join_faces(made, 0, 8, first, True)
    fine_pass(first[...], 1, scale_f, work)
    made = send_faces(1, 1, 8, work, 16, False)

    put_scales(scale_ref, em_ref, 4, scale_m, inv_m)
    pm, pm_t = tables_of(pm_ref, True)
    value = right_table(pm, 4, 8, joined=True, weigh_input=True)
    put_right(right_rf, 0, value[:128])
    put_right(right_rf, 1, value[128:])
    put_left(left_rf, 0, left_table(pm_t, 4, 8, 2, joined=True, weigh_input=True))

    def put_mid(at, table, turned, weighted):
        put_right(right_m, 2 * at, right_table(table, 4, 4))
        put_left_twice(left_m, 2 * at, left_table(turned, 4, 4, 4, copies=2))
        put_right(right_m, 2 * at + 1, right_table(turned, 4, 4, joined=True, weighted=weighted))
        value = left_table(table, 4, 4, 4, joined=True, weighted=weighted, copies=2)
        put_left_twice(left_m, 2 * at + 1, value)

    basis, basis_t = tables_of(bm_ref)
    put_mid(0, basis, basis_t, True)

    join_faces(made, 1, 8, work, False)
    fine_pass(res[...] - work[...], 0, inv_f, second)
    made = send_faces(2, 2, 8, second, 16, True)

    oper, oper_t = tables_of(qm_ref)
    put_mid(1, oper, oper_t, False)
    put_scales(scale_ref, el_ref, 2, None, inv_l)

    join_faces(made, 2, 8, second, True)
    first[...] = first[...] + second[...]
    fine_pass(first[...], 1, scale_f, work)
    made = send_faces(3, 3, 8, work, 16, False)

    plow, plow_t = tables_of(plow_ref, True)
    value = right_table(plow, 2, 4, joined=True, weigh_input=True, copies=2)
    high, low = split(value)
    value = jnp.where(iota(value.shape, 1) < 64, high.astype(F32), low.astype(F32)).astype(BF)
    right_rm[0, 0:128] = value
    right_rm[0, 128:256] = value
    value = left_table(plow_t, 2, 4, 4, joined=True, weigh_input=True, copies=2)
    put_left_twice(left_rm, 0, value)
    basis, basis_t = tables_of(bl_ref)
    put_pair(right_l, 0, right_table(basis, 2, 2))
    put_pair(left_l, 0, left_table(basis_t, 2, 2, EZ))
    put_pair(right_l, 1, right_table(basis_t, 2, 2, joined=True, weighted=True))
    put_pair(left_l, 1, left_table(basis, 2, 2, EZ, joined=True, weighted=True))

    join_faces(made, 3, 8, work, False)

    def ends_weighed(x, n):
        planes = x.shape[0]
        return jnp.concatenate(
            [
                x[0:1] * weight_low_end, x[1 : n - 1], x[n - 1 : n + 1] * 0.5,
                x[n + 1 : planes - 1], x[planes - 1 :] * weight_high_end,
            ],
            0,
        )

    blocks = cut_rows(ends_weighed(res[...] - work[...], 8), 8, 16)
    x = paste_rows(wide_left(left_rf[0], blocks[:6]) + wide_left(left_rf[0], blocks[6:]), 4)
    x = x.reshape(384, 256)
    x = wide_right(x[:, :128], right_rf[0]) + wide_right(x[:, 128:], right_rf[1])
    rhs_m[...] = x.reshape(8, 48, 128)
    made = send_faces(4, 0, 4, rhs_m, 8, False)

    route = route_ref[...]
    hot = picked(iota((64, 768), 0) == route)
    target_hot[...] = hot.astype(BF)
    earlier = picked(iota((768, 768), 0) < iota((768, 768), 1)).astype(BF)
    rank = jnp.sum(mm(target_hot[...], earlier) * hot, axis=0, keepdims=True)
    slot_hot[...] = picked(iota((128, 768), 0).astype(F32) == rank)
    half = jnp.where(rank >= HALF_CAP, 1.0, 0.0)
    owner = 2 * route + jnp.where(rank >= HALF_CAP, 1, 0)
    owner = lax.rem(owner, n_azim) * n_axial + owner // n_azim
    row_hot[...] = picked(iota((128, 768), 0) == owner).astype(BF)
    place_hot[...] = picked(iota((16, 768), 0).astype(F32) == rank - HALF_CAP * half)

    join_faces(made, 0, 4, rhs_m, False)

    def mid_pass(x, which, factor):
        for at in (2 * which, 2 * which + 1):
            x = wide_right(x.reshape(384, 128), right_m[at]).reshape(8, 48, 128)
            x = paste_rows(wide_left(left_m[at], cut_rows(x, 4, 16)), 4)
            if at == 2 * which:
                x = x * factor[...]
        return x

    smooth_m[...] = mid_pass(rhs_m[...], 0, inv_m)
    made = send_faces(5, 1, 4, smooth_m, 16, True)
    put_right(right_pf, 0, right_table(pm_t, 8, 4))
    put_left_thrice(left_pf, 0, left_table(pm, 8, 4, 4, copies=3))
    join_faces(made, 1, 4, smooth_m, True)

    work_m[...] = mid_pass(smooth_m[...], 1, scale_m)
    made = send_faces(6, 2, 4, work_m, 16, False)
    both = jnp.zeros((8, 128), F32)
    both_t = jnp.zeros((8, 128), F32)
    for k in range(4):
        both = both + pm[:, k : k + 1] * plow[k : k + 1, :]
        both_t = both_t + plow_t[:, k : k + 1] * pm_t[k : k + 1, :]
    put_pair(right_pp, 0, right_table(both_t, 8, 2))
    put_left_thrice(left_pp, 0, left_table(both, 8, 2, 4, copies=3))
    join_faces(made, 2, 4, work_m, False)

    blocks = cut_rows(ends_weighed(rhs_m[...] - work_m[...], 4), 4, 16)
    x = paste_rows(wide_left(left_rm[0], blocks), 2).reshape(96, 128)
    rhs_l[...] = wide_right(x, right_rm[0]).reshape(4, 24, 64)
    made = send_faces(7, 0, 2, rhs_l, 8, False)

    slot = iota((128, 3072), 0)
    lane = iota((1, 3072), 1)
    half_lane = jnp.where(lane >= 1536, 1, 0)
    rest = lane - 1536 * half_lane
    source = jnp.floor((rest.astype(F32) + 0.5) * (1.0 / HALF_CAP)).astype(jnp.int32)
    wanted = half_lane * HALF_CAP + rest - source * HALF_CAP
    sel_hot[...] = picked(slot == wanted).astype(BF)
    join_faces(made, 0, 2, rhs_l, False)

    values = []
    lane = iota((24, 384), 1)
    mine = iota((24, 384), 0) == 2 * (lane >> 5)
    pick_r = picked(iota((64, 384), 0) == 2 * (iota((64, 384), 1) & 31))
    for a in range(2):
        wide = jnp.dot(rhs_l[2 * a], pick_r, precision=HIGHEST, preferred_element_type=F32)
        values.append(jnp.sum(jnp.where(mine, wide, 0.0), axis=0, keepdims=True))
    values = jnp.concatenate(values, 1)
    high, low = split(slot_hot[...] * values)
    nt = (((1,), (1,)), ((), ()))
    flat_a[...] = lax.dot_general(
        target_hot[...], high, nt, preferred_element_type=F32
    ) + lax.dot_general(target_hot[...], low, nt, preferred_element_type=F32)
    for t in range(64):
        send_a[t % 2, t // 2] = flat_a[t : t + 1]

    def across(count, copy_to, sem):
        def start(j, carry):
            source, target, device = copy_to(j)
            pltpu.make_async_remote_copy(
                src_ref=source, dst_ref=target,
                send_sem=all_sem.at[sem], recv_sem=all_sem.at[sem + 1],
                device_id=device, device_id_type=MESH,
            ).start()
            return carry

        lax.fori_loop(1, count, start, 0)

    def wait_all(target, count, sem):
        some = target.at[pl.ds(0, count - 1)]
        pltpu.make_async_copy(some, some, all_sem.at[sem]).wait()

    def first_out(j):
        other = lax.rem(me_z + j, n_azim)
        return send_a.at[other // 2], stage_a.at[me_z], (me_a, other)

    across(n_azim, first_out, 0)
    stage_a[me_z] = send_a[me_z // 2]

    def low_pass(x, factor):
        for side in range(2):
            y = mm_right(x.reshape(96, 64), right_l.at[side]).reshape(2, 48, 64)
            x = jnp.concatenate(
                [mm_left(left_l.at[side], y[a]).reshape(2, 24, 64) for a in range(2)], 0
            )
            if side == 0:
                x = x * factor[...]
        return x

    smooth_l[...] = low_pass(rhs_l[...], inv_l)
    made = send_faces(8, 1, 2, smooth_l, None, True)
    wait_all(stage_a, n_azim, 1)

    def second_out(j):
        other = lax.rem(me_a + j, n_axial)
        return stage_a.at[:, other], recv_a.at[me_a], (other, me_z)

    across(n_axial, second_out, 2)
    recv_a[me_a] = stage_a[:, me_a]

    x = wide_right(smooth_m[...].reshape(384, 128), right_pf[0]).reshape(8, 48, 256)
    x = paste_rows(thrice_left(left_pf[0], cut_rows(x, 4, 16)), 8)
    out_ref[...] = first[...] + x
    join_faces(made, 1, 2, smooth_l, True)

    wait_all(recv_a, n_axial, 3)
    for d in range(devices):
        flat_b[d : d + 1] = recv_a[d // n_azim, d % n_azim]
    high, low = split(flat_b[...])
    wide = mm(high, sel_hot[...]) + mm(low, sel_hot[...])
    wide = jnp.where(iota((128, 3072), 0) == source, wide, 0.0)
    vector[...] = jnp.broadcast_to(jnp.sum(wide, axis=0, keepdims=True), (8, 3072))
    load_dense.wait()

    def rows_of(r, carry):
        base = pl.multiple_of(r * 32, 32)
        sums = [None] * 4
        for c in range(24):
            v = vector[:, c * 128 : (c + 1) * 128]
            for k in range(4):
                term = dense[pl.ds(base + 8 * k, 8), c * 128 : (c + 1) * 128] * v
                sums[k] = term if sums[k] is None else sums[k] + term
        for k in range(4):
            partial[pl.ds(base + 8 * k, 8), :] = sums[k]
        return carry

    lax.fori_loop(0, 48, rows_of, 0)
    high, low = split(partial[...])
    ones = jnp.ones((128, 128), BF)
    sums = mm(high, ones) + mm(low, ones)
    row = iota((1536, 128), 0)
    group = jnp.floor((row.astype(F32) + 0.5) * (1.0 / HALF_CAP)).astype(jnp.int32)
    sums = jnp.where(iota((1536, 128), 1) == row - group * HALF_CAP, sums, 0.0)
    high, low = split(sums)
    lane = iota((1, 1536), 1)
    group = jnp.floor((lane.astype(F32) + 0.5) * (1.0 / HALF_CAP)).astype(jnp.int32)
    gather = picked(iota((128, 1536), 0) == group).astype(BF)
    flat_b[...] = mm(gather, high) + mm(gather, low)
    for d in range(devices):
        send_b[d // n_azim, d % n_azim] = flat_b[d : d + 1]

    def first_back(j):
        other = lax.rem(me_a + j, n_axial)
        return send_b.at[other], stage_b.at[me_a], (other, me_z)

    across(n_axial, first_back, 4)
    stage_b[me_a] = send_b[me_a]
    wait_all(stage_b, n_axial, 5)

    def second_back(j):
        other = lax.rem(me_z + j, n_azim)
        return stage_b.at[:, other], recv_b.at[me_z], (me_a, other)

    across(n_azim, second_back, 6)
    recv_b[me_z] = stage_b[:, me_z]
    wait_all(recv_b, n_azim, 7)
    for d in range(devices):
        flat_b[d : d + 1] = recv_b[d // n_axial, d % n_axial]

    turned = jnp.transpose(flat_b[...])[0:16]
    high, low = split(turned)
    answers = mm(high, row_hot[...]) + mm(low, row_hot[...])
    answers = jnp.sum(answers * place_hot[...], axis=0, keepdims=True)
    row = iota((24, 384), 0)
    belongs = (iota((24, 384), 1) >> 5) == ((row + 1) >> 1)
    to_lanes = picked(
        (iota((384, 64), 0) & 31) == ((iota((384, 64), 1) + 1) >> 1)
    ).astype(BF)
    grids = []
    for a in range(2):
        high, low = split(jnp.where(belongs, answers[:, a * 384 : (a + 1) * 384], 0.0))
        grids.append(mm(high, to_lanes) + mm(low, to_lanes))
    cs_plane[...] = grids[0]
    cs_row[0] = grids[0][0:1]
    cs_row[1] = grids[1][0:1]
    made = []
    for k, (source, target, da, dz) in enumerate((
        (cs_plane, cr_plane, -1, 0),
        (cs_row, cr_row.at[pl.ds(0, 2)], 0, -1),
        (cs_row.at[0], cr_row.at[2], -1, -1),
    )):
        copy = pltpu.make_async_remote_copy(
            src_ref=source, dst_ref=target,
            send_sem=send_sem.at[9, k], recv_sem=recv_sem.at[9, k],
            device_id=neighbour(da, dz), device_id_type=MESH,
        )
        copy.start()
        made.append(copy)
    pending.extend(made)
    for copy in made:
        copy.wait_recv()
    last_row = iota((24, 64), 0) == 23
    lower = jnp.where(last_row, cr_row[0], grids[0])
    upper = jnp.where(last_row, cr_row[1], grids[1])
    beyond = jnp.where(last_device, 0.0, jnp.where(last_row, cr_row[2], cr_plane[...]))
    total_l[0] = smooth_l[0] + lower
    total_l[1] = smooth_l[1] + upper
    total_l[2] = smooth_l[2] + upper
    total_l[3] = smooth_l[3] + beyond

    wide = mm_right(total_l[...].reshape(96, 64), right_pp.at[0]).reshape(4, 24, 256)
    out_ref[...] += paste_rows(thrice_left(left_pp[0], cut_rows(wide, 2, 8)), 8)

    for copy in pending:
        copy.wait_send()
    wait_all(stage_a, n_azim, 0)
    wait_all(recv_a, n_axial, 2)
    wait_all(stage_b, n_axial, 4)
    wait_all(recv_b, n_azim, 6)


def on_device(
    residual, element_scale, basis_fine, eigen_fine, operator_fine, basis_mid, eigen_mid,
    operator_mid, basis_low, eigen_low, prolong_mid, prolong_low, vertex_route, coarse_inverse,
):
    def vm(*shape, dtype=F32):
        return pltpu.VMEM(shape, dtype)

    def face_buffers(count, planes, rows, lanes):
        return [
            vm(count, 2, rows, lanes), vm(count, 2, rows, lanes),
            vm(count, 2, planes, lanes), vm(count, 2, planes, lanes),
            vm(count, 4, 1, lanes), vm(count, 4, 1, lanes),
        ]

    fine, mid, low = (16, 96, 256), (8, 48, 128), (4, 24, 64)
    scratch = [
        vm(*fine), vm(*fine), vm(*fine), vm(*fine), vm(*fine), vm(*fine),
        vm(*mid), vm(*mid), vm(*mid), vm(*mid), vm(*mid),
        vm(*low), vm(*low), vm(*low), vm(*low),
        vm(8, 256, 256, dtype=BF), vm(4, 256, 256, dtype=BF),
        vm(2, 256, 256, dtype=BF), vm(1, 64, 256, dtype=BF),
        vm(1, 256, 512, dtype=BF), vm(1, 256, 192, dtype=BF),
        vm(4, 256, 256, dtype=BF), vm(4, 128, 128, dtype=BF),
        vm(1, 256, 128, dtype=BF), vm(1, 32, 128, dtype=BF),
        vm(2, 2, 64, 64, dtype=BF), vm(2, 2, 48, 48, dtype=BF),
        vm(1, 2, 64, 256, dtype=BF), vm(1, 256, 48, dtype=BF),
        vm(1536, 3072), vm(64, 768, dtype=BF), vm(128, 768), vm(128, 768, dtype=BF),
        vm(16, 768), vm(128, 3072, dtype=BF), vm(8, 3072), vm(1536, 128),
        vm(64, 128), vm(2, 32, 1, 128), vm(4, 32, 1, 128), vm(32, 4, 1, 128),
        vm(128, 128), vm(32, 4, 1, 128), vm(32, 4, 1, 128), vm(4, 32, 1, 128),
        vm(24, 64), vm(2, 1, 64), vm(24, 64), vm(3, 1, 64),
        *face_buffers(4, *fine), *face_buffers(3, *mid), *face_buffers(2, *low),
        pltpu.SemaphoreType.DMA((10, 8)), pltpu.SemaphoreType.DMA((10, 8)),
        pltpu.SemaphoreType.DMA((2,)), pltpu.SemaphoreType.DMA((8,)),
    ]
    in_vmem = pl.BlockSpec(memory_space=pltpu.VMEM)
    in_smem = pl.BlockSpec(memory_space=pltpu.SMEM)
    anywhere = pl.BlockSpec(memory_space=pl.ANY)
    call = pl.pallas_call(
        functools.partial(
            kernel, n_axial=lax.axis_size("axial"), n_azim=lax.axis_size("azim")
        ),
        out_shape=jax.ShapeDtypeStruct(residual.shape, F32),
        in_specs=[anywhere, in_vmem, in_vmem, anywhere] + [in_smem] * 10,
        out_specs=in_vmem,
        scratch_shapes=scratch,
        compiler_params=pltpu.CompilerParams(
            collective_id=0, has_side_effects=True, vmem_limit_bytes=58 * 1024 * 1024
        ),
        cost_estimate=pl.CostEstimate(
            flops=12_000_000_000, bytes_accessed=24_000_000, transcendentals=0
        ),
    )
    return call(
        residual, jnp.transpose(element_scale, (0, 2, 1, 3)), vertex_route.reshape(1, -1), coarse_inverse,
        basis_fine, eigen_fine, operator_fine, basis_mid, eigen_mid, operator_mid,
        basis_low, eigen_low, prolong_mid.T, prolong_low.T,
    )


def solution(mesh):
    return jax.shard_map(
        on_device,
        mesh=mesh,
        in_specs=(
            P("axial", "azim", None),
            P(None, "axial", "azim", None),
            P(), P(), P(), P(), P(), P(), P(), P(), P(), P(),
            P("axial", "azim", None, None),
            P("axial", "azim", None, None),
        ),
        out_specs=P("axial", "azim", None),
        check_vma=False,
    )
```

```python
import functools

import jax
import jax.numpy as jnp
from jax import lax
from jax.experimental import pallas as pl
from jax.experimental.pallas import tpu as pltpu
from jax.sharding import PartitionSpec as P

F32 = jnp.float32
BF = jnp.bfloat16
HIGHEST = lax.Precision.HIGHEST
MESH = pl.DeviceIdType.MESH

EZ, ER = 12, 32
HALF_CAP = 12
DIRS = ((1, 0), (-1, 0), (0, 1), (0, -1), (1, 1), (1, -1), (-1, 1), (-1, -1))


def iota(shape, dim):
    return lax.broadcasted_iota(jnp.int32, shape, dim)


def split(x):
    high = x.astype(BF)
    return high, (x - high.astype(F32)).astype(BF)


def mm(a, b):
    return jnp.dot(a, b, preferred_element_type=F32)


def mm_right(x, table):
    high, low = split(x)
    return mm(high, table[0]) + mm(high, table[1]) + mm(low, table[0])


def mm_left(table, x):
    high, low = split(x)
    return mm(table[0], high) + mm(table[1], high) + mm(table[0], low)


def wide_right(x, table):
    high, low = split(x)
    both = mm(jnp.concatenate([high, low], 1), table)
    size = table.shape[1] // 2
    return both[:, :size] + both[:, size:]


def wide_left(table, blocks):
    high, low = split(jnp.concatenate(blocks, 1))
    both = mm(table, jnp.concatenate([high, low], 0))
    size = table.shape[0] // 2
    both = both[:size] + both[size:]
    lanes = blocks[0].shape[1]
    return [both[:, k * lanes : (k + 1) * lanes] for k in range(len(blocks))]


def thrice_left(table, blocks):
    high, low = split(jnp.concatenate(blocks, 1))
    both = mm(table, jnp.concatenate([high, high, low], 0))
    lanes = blocks[0].shape[1]
    return [both[:, k * lanes : (k + 1) * lanes] for k in range(len(blocks))]


def cut_rows(x, n, rows):
    planes, length, lanes = x.shape
    return [
        x[a * n : a * n + n, r : r + rows].reshape(n * rows, lanes)
        for a in range(planes // n)
        for r in range(0, length, rows)
    ]


def paste_rows(blocks, n):
    rows, lanes = blocks[0].shape[0] // n, blocks[0].shape[1]
    half = len(blocks) // 2
    blocks = [b.reshape(n, rows, lanes) for b in blocks]
    return jnp.concatenate(
        [jnp.concatenate(blocks[:half], 1), jnp.concatenate(blocks[half:], 1)], 0
    )


def picked(condition):
    return jnp.where(condition, 1.0, 0.0).astype(F32)


def quotient(x, size, count):
    if size & (size - 1) == 0:
        return x >> (size.bit_length() - 1)
    total = jnp.zeros_like(x)
    for k in range(1, count):
        total = total + jnp.where(x >= size * k, 1, 0)
    return total


def tables_of(ref, turned_in=False):
    n, m = ref.shape if turned_in else ref.shape[::-1]
    row, lane = iota((8, 128), 0), iota((8, 128), 1)
    plain = jnp.where(lane < 8, row * 8 + lane, -1)
    turned = jnp.where(lane < 8, lane * 8 + row, -1)
    table = jnp.zeros((8, 128), F32)
    transposed = jnp.zeros((8, 128), F32)
    for i in range(m):
        for j in range(n):
            value = ref[j, i] if turned_in else ref[i, j]
            table = jnp.where(plain == i * 8 + j, value, table)
            transposed = jnp.where(turned == i * 8 + j, value, transposed)
    return table, transposed


def spread_columns(table, count, length, place):
    index = place(iota((8, length), 1))
    result = jnp.zeros((8, length), F32)
    for j in range(count):
        result = jnp.where(index == j, table[:, j : j + 1], result)
    return result


def spread_rows(table, length, place):
    high = table.astype(BF).astype(F32)
    rest = table - high
    middle = rest.astype(BF).astype(F32)
    pieces = jnp.concatenate([high, middle, rest - middle], 0).astype(BF)
    index = place(iota((length, 24), 0))
    return mm(picked((iota((length, 24), 1) & 7) == index).astype(BF), pieces)


def left_table(table, m, n, group, joined=False, weighted=False, weigh_input=False, copies=1):
    rows, columns = m * group * m, n * group * n

    def once(x):
        return x if copies == 1 else x - columns * quotient(x, columns, copies)

    def parts(x, nodes):
        outer = quotient(x, group * nodes, nodes)
        inner = x - outer * (group * nodes)
        block = quotient(inner, nodes, group)
        return outer, block, inner - block * nodes

    first = spread_columns(table, n, copies * columns, lambda x: parts(once(x), n)[0])
    second = spread_columns(table, n, copies * columns, lambda x: parts(once(x), n)[2])
    outer = spread_rows(first, rows, lambda x: parts(x, m)[0])
    inner = spread_rows(second, rows, lambda x: parts(x, m)[2])
    shape = (rows, copies * columns)
    _, row_block, q = parts(iota(shape, 0), m)
    _, column_block, j = parts(once(iota(shape, 1)), n)
    value = jnp.where(row_block == column_block, inner, 0.0)
    if joined:
        value = value + jnp.where(
            (q == m - 1) & (row_block + 1 == column_block), second[0:1], 0.0
        )
        value = value + jnp.where(
            (q == 0) & (row_block - 1 == column_block), second[m - 1 : m], 0.0
        )
    if weighted:
        value = jnp.where((q == 0) | (q == m - 1), 0.5 * value, value)
    if weigh_input:
        value = jnp.where((j == 0) | (j == n - 1), 0.5 * value, value)
    return outer * value


def right_table(
    turned, m, n, count=ER, joined=False, weighted=False, weigh_input=False,
    first=True, last=True, copies=1,
):
    rows, columns = count * n, count * m
    spread = spread_columns(turned, m, copies * columns, lambda x: x & (m - 1))
    inner = spread_rows(spread, rows, lambda x: x & (n - 1))
    shape = (rows, copies * columns)
    row, column = iota(shape, 0), iota(shape, 1) & (columns - 1)
    row_block, k = quotient(row, n, count), row & (n - 1)
    column_block, s = quotient(column, m, count), column & (m - 1)
    value = jnp.where(row_block == column_block, inner, 0.0)
    if joined:
        value = value + jnp.where(
            (s == m - 1) & (column_block + 1 == row_block), inner[:, 0:1], 0.0
        )
        value = value + jnp.where(
            (s == 0) & (column_block - 1 == row_block), inner[:, m - 1 : m], 0.0
        )

    def halved(place, block, nodes, value):
        low, high = place == 0, place == nodes - 1
        if first:
            low = low & (block > 0)
        if last:
            high = high & (block < count - 1)
        return jnp.where(low | high, 0.5 * value, value)

    if weighted:
        value = halved(s, column_block, m, value)
    if weigh_input:
        value = halved(k, row_block, n, value)
    return value


def put_pair(ref, index, value):
    high, low = split(value)
    ref[index, 0] = high
    ref[index, 1] = low


def put_right(ref, index, value):
    rows, columns = value.shape
    high, low = split(value)
    for k in range(2):
        ref[index, k * rows : (k + 1) * rows, 0:columns] = high
        ref[index, k * rows : (k + 1) * rows, columns : 2 * columns] = low


def put_left(ref, index, value):
    rows, columns = value.shape
    high, low = split(value)
    for k in range(2):
        ref[index, 0:rows, k * columns : (k + 1) * columns] = high
        ref[index, rows : 2 * rows, k * columns : (k + 1) * columns] = low


def put_left_twice(ref, index, value):
    rows = value.shape[0]
    high, low = split(value)
    ref[index, 0:rows] = high
    ref[index, rows : 2 * rows] = low


def put_left_thrice(ref, index, value):
    columns = value.shape[1] // 3
    high, low = split(value)
    lane = iota(value.shape, 1)
    middle = (lane >= columns) & (lane < 2 * columns)
    ref[index] = jnp.where(middle, low.astype(F32), high.astype(F32)).astype(BF)


def put_scales(scale_ref, eig_ref, n, scale_out, inverse_out):
    rows, lanes = EZ * n, ER * n
    spread_z = picked(quotient(iota((rows, EZ), 0), n, EZ) == iota((rows, EZ), 1))
    spread_r = picked(iota((ER, lanes), 0) == quotient(iota((ER, lanes), 1), n, ER))
    row = iota((rows, lanes), 0) & (n - 1)
    lane = iota((rows, lanes), 1) & (n - 1)
    eig_row = jnp.zeros((rows, lanes), F32)
    eig_lane = jnp.zeros((rows, lanes), F32)
    for k in range(n):
        eig_row = jnp.where(row == k, eig_ref[k], eig_row)
        eig_lane = jnp.where(lane == k, eig_ref[k], eig_lane)
    for a in range(2):
        h = []
        for d in range(3):
            wide = jnp.dot(
                scale_ref[d, :, a], spread_r, precision=HIGHEST, preferred_element_type=F32
            )
            h.append(
                jnp.dot(spread_z, wide, precision=HIGHEST, preferred_element_type=F32)
            )
        flat = h[1] * eig_row + h[2] * eig_lane
        for i in range(n):
            total = h[0] * eig_ref[i] + flat
            if scale_out is not None:
                scale_out[a * n + i] = total
            inverse_out[a * n + i] = 1.0 / total


def kernel(
    res_hbm, scale_ref, route_ref, inverse_hbm,
    bf_ref, ef_ref, qf_ref, bm_ref, em_ref, qm_ref, bl_ref, el_ref, pm_ref, plow_ref,
    out_ref,
    res, first, second, work, scale_f, inv_f, rhs_m, smooth_m, work_m, scale_m, inv_m,
    rhs_l, smooth_l, inv_l, total_l,
    right_f, left_f, right_rf, left_rf, right_pf, left_pf,
    right_m, left_m, right_rm, left_rm, right_l, left_l, right_pp, left_pp,
    dense, target_hot, slot_hot, row_hot, place_hot, sel_hot, vector, partial,
    flat_a, send_a, recv_a, flat_b, send_b, recv_b, cs_plane, cs_row, cr_plane, cr_row,
    hold_f, hold_m, hold_l,
    fs_ax, fr_ax, fs_az, fr_az, fs_dg, fr_dg,
    ms_ax, mr_ax, ms_az, mr_az, ms_dg, mr_dg,
    ls_ax, lr_ax, ls_az, lr_az, ls_dg, lr_dg,
    send_sem, recv_sem, load_sem, all_sem, word_sem,
    *, n_axial, n_azim,
):
    devices = n_axial * n_azim
    me_a, me_z = lax.axis_index("axial"), lax.axis_index("azim")
    me = me_a * n_azim + me_z

    def neighbour(da, dz):
        return (lax.rem(me_a + n_axial + da, n_axial), lax.rem(me_z + n_azim + dz, n_azim))

    load_res = pltpu.make_async_copy(res_hbm, res, load_sem.at[0])
    load_res.start()
    load_dense = pltpu.make_async_copy(inverse_hbm.at[0, 0], dense, load_sem.at[1])
    load_dense.start()

    barrier = pltpu.get_barrier_semaphore()

    for j in range(1, n_axial):
        other = (lax.rem(me_a + j, n_axial), me_z)
        pl.semaphore_signal(barrier, inc=1, device_id=other, device_id_type=MESH)
    for j in range(1, n_azim):
        other = (me_a, lax.rem(me_z + j, n_azim))
        pl.semaphore_signal(barrier, inc=1, device_id=other, device_id_type=MESH)
    for da, dz in DIRS[4:]:
        pl.semaphore_signal(barrier, inc=1, device_id=neighbour(da, dz), device_id_type=MESH)

    def spread_word():
        pl.semaphore_wait(barrier, n_axial - 1 + n_azim - 1 + 4)
        for j in range(1, n_azim):
            other = (me_a, lax.rem(me_z + j, n_azim))
            pl.semaphore_signal(word_sem, inc=1, device_id=other, device_id_type=MESH)

    first_device, last_device = me_a == 0, me_a == n_axial - 1
    weight_low_end = jnp.where(first_device, 1.0, 0.5).astype(F32)
    weight_high_end = jnp.where(last_device, 1.0, 0.5).astype(F32)

    faces = {
        8: (fs_ax, fr_ax, fs_az, fr_az, fs_dg, fr_dg),
        4: (ms_ax, mr_ax, ms_az, mr_az, ms_dg, mr_dg),
        2: (ls_ax, lr_ax, ls_az, lr_az, ls_dg, lr_dg),
    }
    pending = []

    def copies_of(e, slot, n):
        s_ax, r_ax, s_az, r_az, s_dg, r_dg = faces[n]
        made = []
        for d, (da, dz) in enumerate(DIRS):
            if d < 2:
                source, target = s_ax.at[slot, d], r_ax.at[slot, d]
            elif d < 4:
                source, target = s_az.at[slot, d - 2], r_az.at[slot, d - 2]
            else:
                source, target = s_dg.at[slot, d - 4], r_dg.at[slot, d - 4]
            made.append(
                pltpu.make_async_remote_copy(
                    src_ref=source, dst_ref=target,
                    send_sem=send_sem.at[e, d], recv_sem=recv_sem.at[e, d],
                    device_id=neighbour(da, dz), device_id_type=MESH,
                )
            )
        return made

    def send_faces(e, slot, n, buf, step, weighted):
        planes, rows, _ = buf.shape
        if step is not None:
            for at in range(step, rows, step):
                both = buf[:, at - 1 : at, :] + buf[:, at : at + 1, :]
                buf[:, at - 1 : at, :] = both
                buf[:, at : at + 1, :] = both
        both = buf[n - 1] + buf[n]
        if weighted:
            both = 0.5 * both
        buf[n - 1] = both
        buf[n] = both
        s_ax, _, s_az, _, s_dg, _ = faces[n]
        s_ax[slot, 0] = buf[planes - 1]
        s_ax[slot, 1] = buf[0]
        s_dg[slot, 0] = buf[planes - 1, rows - 1 : rows]
        s_dg[slot, 1] = buf[planes - 1, 0:1]
        s_dg[slot, 2] = buf[0, rows - 1 : rows]
        s_dg[slot, 3] = buf[0, 0:1]
        for i in range(planes):
            s_az[slot, 0, i : i + 1] = buf[i, rows - 1 : rows]
            s_az[slot, 1, i : i + 1] = buf[i, 0:1]
        made = copies_of(e, slot, n)
        for copy in made[4:] + made[:4]:
            copy.start()
        pending.extend(made)
        return made

    def join_faces(made, slot, n, buf, weighted):
        planes, rows, _ = buf.shape
        _, r_ax, _, r_az, _, _ = faces[n]
        for copy in made[:4]:
            copy.wait_recv()
        for i in range(planes):
            buf[i, 0:1] = buf[i, 0:1] + r_az[slot, 0, i : i + 1]
            buf[i, rows - 1 : rows] = buf[i, rows - 1 : rows] + r_az[slot, 1, i : i + 1]
        for end, plane, device, weight in (
            (0, 0, first_device, weight_low_end),
            (1, planes - 1, last_device, weight_high_end),
        ):
            total = buf[plane] + jnp.where(device, 0.0, r_ax[slot, end])
            buf[plane] = total * weight if weighted else total

    def join_corners(made, slot, n, buf, weighted):
        r_dg, hold = faces[n][5], holds[n]
        for copy in made[4:]:
            copy.wait_recv()
        for k in range(4):
            end = k // 2
            line = jnp.where((first_device, last_device)[end], 0.0, r_dg[slot, k])
            if weighted:
                line = line * (weight_low_end, weight_high_end)[end]
            hold[k : k + 1] = line
            if buf is not None:
                plane, row = (0, buf.shape[0] - 1)[end], (0, buf.shape[1] - 1)[k % 2]
                buf[plane, row : row + 1] = buf[plane, row : row + 1] + line
        return hold[...]

    def add_corners(blocks, table, columns, lines):
        half, count = table.shape[0] // 2, len(blocks) // 2
        table = table[:, :128].astype(F32)
        for k, column in enumerate(columns):
            at = (0, count - 1, count, 2 * count - 1)[k]
            factor = table[:half, column : column + 1] + table[half:, column : column + 1]
            blocks[at] = blocks[at] + factor * lines[k : k + 1]
        return blocks

    FINE_CORNERS, MID_CORNERS = (0, 15, 112, 127), (0, 15, 48, 63)
    holds = {8: hold_f, 4: hold_m, 2: hold_l}
    for hold in holds.values():
        hold[...] = jnp.zeros(hold.shape, F32)

    def fine_right(x, which, joined):
        planes, rows, lanes = x.shape
        x = x.reshape(planes * rows, lanes)
        left = wide_right(x[:, :128], right_f[2 * which])
        right = wide_right(x[:, 128:], right_f[2 * which + 1])
        if joined:
            lane = iota(left.shape, 1)
            left, right = (
                left + jnp.where(lane == 127, pltpu.roll(right, 127, 1), 0.0),
                right + jnp.where(lane == 0, pltpu.roll(left, 1, 1), 0.0),
            )
        return jnp.concatenate([left, right], 1).reshape(planes, rows, lanes)

    def fine_left(x, which):
        half = 6
        blocks = cut_rows(x, 8, 16)
        table = left_f[which]
        return wide_left(table, blocks[:half]) + wide_left(table, blocks[half:])

    def fine_pass(x, which, factor, result, corners=None):
        z = fine_left(fine_right(x, 2 * which, False), 2 * which)
        if corners is not None:
            lines = fine_right(corners().reshape(1, 16, 256), 2 * which, False).reshape(16, 256)
            z = add_corners(z, left_f[2 * which], FINE_CORNERS, lines)
        z = paste_rows(z, 8) * factor[...]
        z = fine_right(z, 2 * which + 1, True)
        result[...] = paste_rows(fine_left(z, 2 * which + 1), 8)

    basis, basis_t = tables_of(bf_ref)

    def put_fine(at, table, turned, weighted):
        value = right_table(table, 8, 8, 16)
        put_right(right_f, 4 * at, value)
        put_right(right_f, 4 * at + 1, value)
        put_left(left_f, 2 * at, left_table(turned, 8, 8, 2))
        for end in range(2):
            value = right_table(
                turned, 8, 8, 16, joined=True, weighted=weighted, first=end == 0, last=end == 1
            )
            put_right(right_f, 4 * at + 2 + end, value)
        put_left(left_f, 2 * at + 1, left_table(table, 8, 8, 2, joined=True, weighted=weighted))

    put_fine(0, basis, basis_t, True)
    put_scales(scale_ref, ef_ref, 8, scale_f, inv_f)

    load_res.wait()
    fine_pass(res[...], 0, inv_f, first)
    spread_word()
    made = send_faces(0, 0, 8, first, 16, True)

    oper, oper_t = tables_of(qf_ref)
    put_fine(1, oper, oper_t, False)

    join_faces(made, 0, 8, first, True)
    fine_pass(
        first[...], 1, scale_f, work, lambda: join_corners(made, 0, 8, first, True)
    )
    made = send_faces(1, 1, 8, work, 16, False)

    put_scales(scale_ref, em_ref, 4, scale_m, inv_m)
    pm, pm_t = tables_of(pm_ref, True)
    value = right_table(pm, 4, 8, joined=True, weigh_input=True)
    put_right(right_rf, 0, value[:128])
    put_right(right_rf, 1, value[128:])
    put_left(left_rf, 0, left_table(pm_t, 4, 8, 2, joined=True, weigh_input=True))

    def put_mid(at, table, turned, weighted):
        put_right(right_m, 2 * at, right_table(table, 4, 4))
        put_left_twice(left_m, 2 * at, left_table(turned, 4, 4, 4, copies=2))
        put_right(right_m, 2 * at + 1, right_table(turned, 4, 4, joined=True, weighted=weighted))
        value = left_table(table, 4, 4, 4, joined=True, weighted=weighted, copies=2)
        put_left_twice(left_m, 2 * at + 1, value)

    basis, basis_t = tables_of(bm_ref)
    put_mid(0, basis, basis_t, True)

    join_faces(made, 1, 8, work, False)
    fine_pass(
        res[...] - work[...], 0, inv_f, second, lambda: -join_corners(made, 1, 8, work, False)
    )
    made = send_faces(2, 2, 8, second, 16, True)

    oper, oper_t = tables_of(qm_ref)
    put_mid(1, oper, oper_t, False)
    put_scales(scale_ref, el_ref, 2, None, inv_l)

    join_faces(made, 2, 8, second, True)
    first[...] = first[...] + second[...]
    fine_pass(
        first[...], 1, scale_f, work, lambda: join_corners(made, 2, 8, first, True)
    )
    made = send_faces(3, 3, 8, work, 16, False)

    plow, plow_t = tables_of(plow_ref, True)
    value = right_table(plow, 2, 4, joined=True, weigh_input=True, copies=2)
    high, low = split(value)
    value = jnp.where(iota(value.shape, 1) < 64, high.astype(F32), low.astype(F32)).astype(BF)
    right_rm[0, 0:128] = value
    right_rm[0, 128:256] = value
    value = left_table(plow_t, 2, 4, 4, joined=True, weigh_input=True, copies=2)
    put_left_twice(left_rm, 0, value)
    basis, basis_t = tables_of(bl_ref)
    put_pair(right_l, 0, right_table(basis, 2, 2))
    put_pair(left_l, 0, left_table(basis_t, 2, 2, EZ))
    put_pair(right_l, 1, right_table(basis_t, 2, 2, joined=True, weighted=True))
    put_pair(left_l, 1, left_table(basis, 2, 2, EZ, joined=True, weighted=True))

    join_faces(made, 3, 8, work, False)

    def ends_weighed(x, n):
        planes = x.shape[0]
        return jnp.concatenate(
            [
                x[0:1] * weight_low_end, x[1 : n - 1], x[n - 1 : n + 1] * 0.5,
                x[n + 1 : planes - 1], x[planes - 1 :] * weight_high_end,
            ],
            0,
        )

    blocks = cut_rows(ends_weighed(res[...] - work[...], 8), 8, 16)
    blocks = wide_left(left_rf[0], blocks[:6]) + wide_left(left_rf[0], blocks[6:])
    lines = -join_corners(made, 3, 8, None, True)
    x = paste_rows(add_corners(blocks, left_rf[0], FINE_CORNERS, lines), 4)
    x = x.reshape(384, 256)
    x = wide_right(x[:, :128], right_rf[0]) + wide_right(x[:, 128:], right_rf[1])
    rhs_m[...] = x.reshape(8, 48, 128)
    made = send_faces(4, 0, 4, rhs_m, 8, False)

    route = route_ref[...]
    hot = picked(iota((64, 768), 0) == route)
    target_hot[...] = hot.astype(BF)
    earlier = picked(iota((768, 768), 0) < iota((768, 768), 1)).astype(BF)
    rank = jnp.sum(mm(target_hot[...], earlier) * hot, axis=0, keepdims=True)
    slot_hot[...] = picked(iota((128, 768), 0).astype(F32) == rank)
    half = jnp.where(rank >= HALF_CAP, 1.0, 0.0)
    owner = 2 * route + jnp.where(rank >= HALF_CAP, 1, 0)
    row_hot[...] = picked(iota((128, 768), 0) == owner).astype(BF)
    place_hot[...] = picked(iota((16, 768), 0).astype(F32) == rank - HALF_CAP * half)

    join_faces(made, 0, 4, rhs_m, False)

    def mid_right(x, at):
        planes, rows, lanes = x.shape
        return wide_right(x.reshape(planes * rows, lanes), right_m[at]).reshape(x.shape)

    def mid_pass(x, which, factor, corners):
        at = 2 * which
        blocks = wide_left(left_m[at], cut_rows(mid_right(x, at), 4, 16))
        lines = mid_right(corners().reshape(1, 16, 128), at).reshape(16, 128)
        x = paste_rows(add_corners(blocks, left_m[at], MID_CORNERS, lines), 4) * factor[...]
        x = mid_right(x, at + 1)
        return paste_rows(wide_left(left_m[at + 1], cut_rows(x, 4, 16)), 4)

    smooth_m[...] = mid_pass(
        rhs_m[...], 0, inv_m, lambda: join_corners(made, 0, 4, rhs_m, False)
    )
    made = send_faces(5, 1, 4, smooth_m, 16, True)
    put_right(right_pf, 0, right_table(pm_t, 8, 4))
    put_left_thrice(left_pf, 0, left_table(pm, 8, 4, 4, copies=3))
    join_faces(made, 1, 4, smooth_m, True)

    work_m[...] = mid_pass(
        smooth_m[...], 1, scale_m, lambda: join_corners(made, 1, 4, smooth_m, True)
    )
    made = send_faces(6, 2, 4, work_m, 16, False)
    both = jnp.zeros((8, 128), F32)
    both_t = jnp.zeros((8, 128), F32)
    for k in range(4):
        both = both + pm[:, k : k + 1] * plow[k : k + 1, :]
        both_t = both_t + plow_t[:, k : k + 1] * pm_t[k : k + 1, :]
    put_pair(right_pp, 0, right_table(both_t, 8, 2))
    put_left_thrice(left_pp, 0, left_table(both, 8, 2, 4, copies=3))
    join_faces(made, 2, 4, work_m, False)

    blocks = cut_rows(ends_weighed(rhs_m[...] - work_m[...], 4), 4, 16)
    blocks = wide_left(left_rm[0], blocks)
    lines = -join_corners(made, 2, 4, None, True)
    x = paste_rows(add_corners(blocks, left_rm[0], MID_CORNERS, lines), 2).reshape(96, 128)
    rhs_l[...] = wide_right(x, right_rm[0]).reshape(4, 24, 64)
    made = send_faces(7, 0, 2, rhs_l, 8, False)

    slot = iota((128, 3072), 0)
    lane = iota((1, 3072), 1)
    half_lane = jnp.where(lane >= 1536, 1, 0)
    rest = lane - 1536 * half_lane
    source = jnp.floor((rest.astype(F32) + 0.5) * (1.0 / HALF_CAP)).astype(jnp.int32)
    wanted = half_lane * HALF_CAP + rest - source * HALF_CAP
    sel_hot[...] = picked(slot == wanted).astype(BF)
    join_faces(made, 0, 2, rhs_l, False)
    join_corners(made, 0, 2, rhs_l, False)

    values = []
    lane = iota((24, 384), 1)
    mine = iota((24, 384), 0) == 2 * (lane >> 5)
    pick_r = picked(iota((64, 384), 0) == 2 * (iota((64, 384), 1) & 31))
    for a in range(2):
        wide = jnp.dot(rhs_l[2 * a], pick_r, precision=HIGHEST, preferred_element_type=F32)
        values.append(jnp.sum(jnp.where(mine, wide, 0.0), axis=0, keepdims=True))
    values = jnp.concatenate(values, 1)
    high, low = split(slot_hot[...] * values)
    nt = (((1,), (1,)), ((), ()))
    flat_a[...] = lax.dot_general(
        target_hot[...], high, nt, preferred_element_type=F32
    ) + lax.dot_general(target_hot[...], low, nt, preferred_element_type=F32)
    for t in range(64):
        send_a[t] = flat_a[t : t + 1]

    def spread_out(source, row_of, target, sem):
        def start(a, z):
            pltpu.make_async_remote_copy(
                src_ref=source.at[row_of(a, z)], dst_ref=target.at[me],
                send_sem=all_sem.at[sem], recv_sem=all_sem.at[sem + 1],
                device_id=(a, z), device_id_type=MESH,
            ).start()

        around = [lax.rem(me_z + j, n_azim) for j in range(n_azim)]

        def start_line(j, carry):
            a = lax.rem(me_a + j, n_axial)
            for z in around:
                start(a, z)
            return carry

        lax.fori_loop(1, n_axial, start_line, 0)
        for z in around[1:]:
            start(me_a, z)
        target[me] = source[row_of(me_a, me_z)]

    def wait_all(target, sem):
        some = target.at[pl.ds(0, devices - 1)]
        pltpu.make_async_copy(some, some, all_sem.at[sem]).wait()

    pl.semaphore_wait(word_sem, n_azim - 1)
    spread_out(send_a, lambda a, z: a * (n_azim // 2) + z // 2, recv_a, 0)

    def low_pass(x, factor):
        for side in range(2):
            y = mm_right(x.reshape(96, 64), right_l.at[side]).reshape(2, 48, 64)
            x = jnp.concatenate(
                [mm_left(left_l.at[side], y[a]).reshape(2, 24, 64) for a in range(2)], 0
            )
            if side == 0:
                x = x * factor[...]
        return x

    smooth_l[...] = low_pass(rhs_l[...], inv_l)
    made = send_faces(8, 1, 2, smooth_l, None, True)
    wait_all(recv_a, 1)
    for d in range(devices):
        flat_b[d : d + 1] = recv_a[d]
    wide = mm(jnp.concatenate(split(flat_b[...]), 0), sel_hot[...])
    wide = wide[:devices] + wide[devices:]
    wide = jnp.where(iota((128, 3072), 0) == source, wide, 0.0)
    vector[...] = jnp.broadcast_to(jnp.sum(wide, axis=0, keepdims=True), (8, 3072))
    load_dense.wait()

    def rows_of(r, carry):
        base = pl.multiple_of(r * 32, 32)
        sums = [None] * 4
        for c in range(24):
            v = vector[:, c * 128 : (c + 1) * 128]
            for k in range(4):
                term = dense[pl.ds(base + 8 * k, 8), c * 128 : (c + 1) * 128] * v
                sums[k] = term if sums[k] is None else sums[k] + term
        for k in range(4):
            partial[pl.ds(base + 8 * k, 8), :] = sums[k]
        return carry

    lax.fori_loop(0, 48, rows_of, 0)
    sums = mm(jnp.concatenate(split(partial[...]), 1), jnp.ones((256, 128), BF))
    row = iota((1536, 128), 0)
    group = jnp.floor((row.astype(F32) + 0.5) * (1.0 / HALF_CAP)).astype(jnp.int32)
    sums = jnp.where(iota((1536, 128), 1) == row - group * HALF_CAP, sums, 0.0)
    lane = iota((1, 1536), 1)
    group = jnp.floor((lane.astype(F32) + 0.5) * (1.0 / HALF_CAP)).astype(jnp.int32)
    gather = picked(iota((128, 1536), 0) == group).astype(BF)
    both = mm(gather, jnp.concatenate(split(sums), 1))
    flat_b[...] = both[:, :128] + both[:, 128:]
    for d in range(devices):
        send_b[d] = flat_b[d : d + 1]
    spread_out(send_b, lambda a, z: a * n_azim + z, recv_b, 2)

    x = wide_right(smooth_m[...].reshape(384, 128), right_pf[0]).reshape(8, 48, 256)
    x = paste_rows(thrice_left(left_pf[0], cut_rows(x, 4, 16)), 8)
    out_ref[...] = first[...] + x
    join_faces(made, 1, 2, smooth_l, True)
    join_corners(made, 1, 2, smooth_l, True)

    wait_all(recv_b, 3)
    for d in range(devices):
        flat_b[d : d + 1] = recv_b[d]

    turned = jnp.transpose(flat_b[...])[0:16]
    high, low = split(turned)
    answers = mm(high, row_hot[...]) + mm(low, row_hot[...])
    answers = jnp.sum(answers * place_hot[...], axis=0, keepdims=True)
    row = iota((24, 384), 0)
    belongs = (iota((24, 384), 1) >> 5) == ((row + 1) >> 1)
    to_lanes = picked(
        (iota((384, 64), 0) & 31) == ((iota((384, 64), 1) + 1) >> 1)
    ).astype(BF)
    grids = []
    for a in range(2):
        high, low = split(jnp.where(belongs, answers[:, a * 384 : (a + 1) * 384], 0.0))
        grids.append(mm(high, to_lanes) + mm(low, to_lanes))
    cs_plane[...] = grids[0]
    cs_row[0] = grids[0][0:1]
    cs_row[1] = grids[1][0:1]
    made = []
    for k, (source, target, da, dz) in enumerate((
        (cs_plane, cr_plane, -1, 0),
        (cs_row, cr_row.at[pl.ds(0, 2)], 0, -1),
        (cs_row.at[0], cr_row.at[2], -1, -1),
    )):
        copy = pltpu.make_async_remote_copy(
            src_ref=source, dst_ref=target,
            send_sem=send_sem.at[9, k], recv_sem=recv_sem.at[9, k],
            device_id=neighbour(da, dz), device_id_type=MESH,
        )
        copy.start()
        made.append(copy)
    pending.extend(made)
    for copy in made:
        copy.wait_recv()
    last_row = iota((24, 64), 0) == 23
    lower = jnp.where(last_row, cr_row[0], grids[0])
    upper = jnp.where(last_row, cr_row[1], grids[1])
    beyond = jnp.where(last_device, 0.0, jnp.where(last_row, cr_row[2], cr_plane[...]))
    total_l[0] = smooth_l[0] + lower
    total_l[1] = smooth_l[1] + upper
    total_l[2] = smooth_l[2] + upper
    total_l[3] = smooth_l[3] + beyond

    wide = mm_right(total_l[...].reshape(96, 64), right_pp.at[0]).reshape(4, 24, 256)
    out_ref[...] += paste_rows(thrice_left(left_pp[0], cut_rows(wide, 2, 8)), 8)

    for copy in pending:
        copy.wait_send()
    wait_all(recv_a, 0)
    wait_all(recv_b, 2)


def on_device(
    residual, element_scale, basis_fine, eigen_fine, operator_fine, basis_mid, eigen_mid,
    operator_mid, basis_low, eigen_low, prolong_mid, prolong_low, vertex_route, coarse_inverse,
):
    devices = lax.axis_size("axial") * lax.axis_size("azim")

    def vm(*shape, dtype=F32):
        return pltpu.VMEM(shape, dtype)

    def face_buffers(count, planes, rows, lanes):
        return [
            vm(count, 2, rows, lanes), vm(count, 2, rows, lanes),
            vm(count, 2, planes, lanes), vm(count, 2, planes, lanes),
            vm(count, 4, 1, lanes), vm(count, 4, 1, lanes),
        ]

    fine, mid, low = (16, 96, 256), (8, 48, 128), (4, 24, 64)
    scratch = [
        vm(*fine), vm(*fine), vm(*fine), vm(*fine), vm(*fine), vm(*fine),
        vm(*mid), vm(*mid), vm(*mid), vm(*mid), vm(*mid),
        vm(*low), vm(*low), vm(*low), vm(*low),
        vm(8, 256, 256, dtype=BF), vm(4, 256, 256, dtype=BF),
        vm(2, 256, 256, dtype=BF), vm(1, 64, 256, dtype=BF),
        vm(1, 256, 512, dtype=BF), vm(1, 256, 192, dtype=BF),
        vm(4, 256, 256, dtype=BF), vm(4, 128, 128, dtype=BF),
        vm(1, 256, 128, dtype=BF), vm(1, 32, 128, dtype=BF),
        vm(2, 2, 64, 64, dtype=BF), vm(2, 2, 48, 48, dtype=BF),
        vm(1, 2, 64, 256, dtype=BF), vm(1, 256, 48, dtype=BF),
        vm(1536, 3072), vm(64, 768, dtype=BF), vm(128, 768), vm(128, 768, dtype=BF),
        vm(16, 768), vm(128, 3072, dtype=BF), vm(8, 3072), vm(1536, 128),
        vm(64, 128), vm(64, 1, 128), vm(devices, 1, 128),
        vm(devices, 128), vm(devices, 1, 128), vm(devices, 1, 128),
        vm(24, 64), vm(2, 1, 64), vm(24, 64), vm(3, 1, 64),
        vm(16, 256), vm(16, 128), vm(16, 64),
        *face_buffers(4, *fine), *face_buffers(3, *mid), *face_buffers(2, *low),
        pltpu.SemaphoreType.DMA((10, 8)), pltpu.SemaphoreType.DMA((10, 8)),
        pltpu.SemaphoreType.DMA((2,)), pltpu.SemaphoreType.DMA((4,)),
        pltpu.SemaphoreType.REGULAR,
    ]
    in_vmem = pl.BlockSpec(memory_space=pltpu.VMEM)
    in_smem = pl.BlockSpec(memory_space=pltpu.SMEM)
    anywhere = pl.BlockSpec(memory_space=pl.ANY)
    call = pl.pallas_call(
        functools.partial(
            kernel, n_axial=lax.axis_size("axial"), n_azim=lax.axis_size("azim")
        ),
        out_shape=jax.ShapeDtypeStruct(residual.shape, F32),
        in_specs=[anywhere, in_vmem, in_vmem, anywhere] + [in_smem] * 10,
        out_specs=in_vmem,
        scratch_shapes=scratch,
        compiler_params=pltpu.CompilerParams(
            collective_id=0, has_side_effects=True, vmem_limit_bytes=58 * 1024 * 1024
        ),
        cost_estimate=pl.CostEstimate(
            flops=12_000_000_000, bytes_accessed=24_000_000, transcendentals=0
        ),
    )
    return call(
        residual, jnp.transpose(element_scale, (0, 2, 1, 3)), vertex_route.reshape(1, -1), coarse_inverse,
        basis_fine, eigen_fine, operator_fine, basis_mid, eigen_mid, operator_mid,
        basis_low, eigen_low, prolong_mid.T, prolong_low.T,
    )


def solution(mesh):
    return jax.shard_map(
        on_device,
        mesh=mesh,
        in_specs=(
            P("axial", "azim", None),
            P(None, "axial", "azim", None),
            P(), P(), P(), P(), P(), P(), P(), P(), P(), P(),
            P("axial", "azim", None, None),
            P("axial", "azim", None, None),
        ),
        out_specs=P("axial", "azim", None),
        check_vma=False,
    )
```

```python
import functools

import jax
import jax.numpy as jnp
from jax import lax
from jax.experimental import pallas as pl
from jax.experimental.pallas import tpu as pltpu
from jax.sharding import PartitionSpec as P

F32 = jnp.float32
BF = jnp.bfloat16
HIGHEST = lax.Precision.HIGHEST
MESH = pl.DeviceIdType.MESH

EZ, ER = 12, 32
HALF_CAP = 12
DIRS = ((1, 0), (-1, 0), (0, 1), (0, -1), (1, 1), (1, -1), (-1, 1), (-1, -1))


def iota(shape, dim):
    return lax.broadcasted_iota(jnp.int32, shape, dim)


def split(x):
    high = x.astype(BF)
    return high, (x - high.astype(F32)).astype(BF)


def mm(a, b):
    return jnp.dot(a, b, preferred_element_type=F32)


def mm_right(x, table):
    high, low = split(x)
    return mm(high, table[0]) + mm(high, table[1]) + mm(low, table[0])


def mm_left(table, x):
    high, low = split(x)
    return mm(table[0], high) + mm(table[1], high) + mm(table[0], low)


def wide_right(x, table):
    high, low = split(x)
    both = mm(jnp.concatenate([high, low], 1), table)
    size = table.shape[1] // 2
    return both[:, :size] + both[:, size:]


def wide_left(table, blocks):
    high, low = split(jnp.concatenate(blocks, 1))
    both = mm(table, jnp.concatenate([high, low], 0))
    size = table.shape[0] // 2
    both = both[:size] + both[size:]
    lanes = blocks[0].shape[1]
    return [both[:, k * lanes : (k + 1) * lanes] for k in range(len(blocks))]


def thrice_left(table, blocks):
    high, low = split(jnp.concatenate(blocks, 1))
    both = mm(table, jnp.concatenate([high, high, low], 0))
    lanes = blocks[0].shape[1]
    return [both[:, k * lanes : (k + 1) * lanes] for k in range(len(blocks))]


def cut_rows(x, n, rows):
    planes, length, lanes = x.shape
    return [
        x[a * n : a * n + n, r : r + rows].reshape(n * rows, lanes)
        for a in range(planes // n)
        for r in range(0, length, rows)
    ]


def paste_rows(blocks, n):
    rows, lanes = blocks[0].shape[0] // n, blocks[0].shape[1]
    half = len(blocks) // 2
    blocks = [b.reshape(n, rows, lanes) for b in blocks]
    return jnp.concatenate(
        [jnp.concatenate(blocks[:half], 1), jnp.concatenate(blocks[half:], 1)], 0
    )


def picked(condition):
    return jnp.where(condition, 1.0, 0.0).astype(F32)


def quotient(x, size, count):
    if size & (size - 1) == 0:
        return x >> (size.bit_length() - 1)
    total = jnp.zeros_like(x)
    for k in range(1, count):
        total = total + jnp.where(x >= size * k, 1, 0)
    return total


def tables_of(ref, turned_in=False):
    n, m = ref.shape if turned_in else ref.shape[::-1]
    row, lane = iota((8, 128), 0), iota((8, 128), 1)
    plain = jnp.where(lane < 8, row * 8 + lane, -1)
    turned = jnp.where(lane < 8, lane * 8 + row, -1)
    table = jnp.zeros((8, 128), F32)
    transposed = jnp.zeros((8, 128), F32)
    for i in range(m):
        for j in range(n):
            value = ref[j, i] if turned_in else ref[i, j]
            table = jnp.where(plain == i * 8 + j, value, table)
            transposed = jnp.where(turned == i * 8 + j, value, transposed)
    return table, transposed


def spread_columns(table, count, length, place):
    index = place(iota((8, length), 1))
    result = jnp.zeros((8, length), F32)
    for j in range(count):
        result = jnp.where(index == j, table[:, j : j + 1], result)
    return result


def spread_rows(table, length, place):
    high = table.astype(BF).astype(F32)
    rest = table - high
    middle = rest.astype(BF).astype(F32)
    pieces = jnp.concatenate([high, middle, rest - middle], 0).astype(BF)
    index = place(iota((length, 24), 0))
    return mm(picked((iota((length, 24), 1) & 7) == index).astype(BF), pieces)


def left_table(table, m, n, group, joined=False, weighted=False, weigh_input=False, copies=1):
    rows, columns = m * group * m, n * group * n

    def once(x):
        return x if copies == 1 else x - columns * quotient(x, columns, copies)

    def parts(x, nodes):
        outer = quotient(x, group * nodes, nodes)
        inner = x - outer * (group * nodes)
        block = quotient(inner, nodes, group)
        return outer, block, inner - block * nodes

    first = spread_columns(table, n, copies * columns, lambda x: parts(once(x), n)[0])
    second = spread_columns(table, n, copies * columns, lambda x: parts(once(x), n)[2])
    outer = spread_rows(first, rows, lambda x: parts(x, m)[0])
    inner = spread_rows(second, rows, lambda x: parts(x, m)[2])
    shape = (rows, copies * columns)
    _, row_block, q = parts(iota(shape, 0), m)
    _, column_block, j = parts(once(iota(shape, 1)), n)
    value = jnp.where(row_block == column_block, inner, 0.0)
    if joined:
        value = value + jnp.where(
            (q == m - 1) & (row_block + 1 == column_block), second[0:1], 0.0
        )
        value = value + jnp.where(
            (q == 0) & (row_block - 1 == column_block), second[m - 1 : m], 0.0
        )
    if weighted:
        value = jnp.where((q == 0) | (q == m - 1), 0.5 * value, value)
    if weigh_input:
        value = jnp.where((j == 0) | (j == n - 1), 0.5 * value, value)
    return outer * value


def right_table(
    turned, m, n, count=ER, joined=False, weighted=False, weigh_input=False,
    first=True, last=True, copies=1,
):
    rows, columns = count * n, count * m
    spread = spread_columns(turned, m, copies * columns, lambda x: x & (m - 1))
    inner = spread_rows(spread, rows, lambda x: x & (n - 1))
    shape = (rows, copies * columns)
    row, column = iota(shape, 0), iota(shape, 1) & (columns - 1)
    row_block, k = quotient(row, n, count), row & (n - 1)
    column_block, s = quotient(column, m, count), column & (m - 1)
    value = jnp.where(row_block == column_block, inner, 0.0)
    if joined:
        value = value + jnp.where(
            (s == m - 1) & (column_block + 1 == row_block), inner[:, 0:1], 0.0
        )
        value = value + jnp.where(
            (s == 0) & (column_block - 1 == row_block), inner[:, m - 1 : m], 0.0
        )

    def halved(place, block, nodes, value):
        low, high = place == 0, place == nodes - 1
        if first:
            low = low & (block > 0)
        if last:
            high = high & (block < count - 1)
        return jnp.where(low | high, 0.5 * value, value)

    if weighted:
        value = halved(s, column_block, m, value)
    if weigh_input:
        value = halved(k, row_block, n, value)
    return value


def put_pair(ref, index, value):
    high, low = split(value)
    ref[index, 0] = high
    ref[index, 1] = low


def put_right(ref, index, value):
    rows, columns = value.shape
    high, low = split(value)
    for k in range(2):
        ref[index, k * rows : (k + 1) * rows, 0:columns] = high
        ref[index, k * rows : (k + 1) * rows, columns : 2 * columns] = low


def put_left(ref, index, value):
    rows, columns = value.shape
    high, low = split(value)
    for k in range(2):
        ref[index, 0:rows, k * columns : (k + 1) * columns] = high
        ref[index, rows : 2 * rows, k * columns : (k + 1) * columns] = low


def put_left_twice(ref, index, value):
    rows = value.shape[0]
    high, low = split(value)
    ref[index, 0:rows] = high
    ref[index, rows : 2 * rows] = low


def put_left_thrice(ref, index, value):
    columns = value.shape[1] // 3
    high, low = split(value)
    lane = iota(value.shape, 1)
    middle = (lane >= columns) & (lane < 2 * columns)
    ref[index] = jnp.where(middle, low.astype(F32), high.astype(F32)).astype(BF)


def put_scales(scale_ref, eig_ref, n, scale_out, inverse_out):
    rows, lanes = EZ * n, ER * n
    spread_z = picked(quotient(iota((rows, EZ), 0), n, EZ) == iota((rows, EZ), 1))
    spread_r = picked(iota((ER, lanes), 0) == quotient(iota((ER, lanes), 1), n, ER))
    row = iota((rows, lanes), 0) & (n - 1)
    lane = iota((rows, lanes), 1) & (n - 1)
    eig_row = jnp.zeros((rows, lanes), F32)
    eig_lane = jnp.zeros((rows, lanes), F32)
    for k in range(n):
        eig_row = jnp.where(row == k, eig_ref[k], eig_row)
        eig_lane = jnp.where(lane == k, eig_ref[k], eig_lane)
    for a in range(2):
        h = []
        for d in range(3):
            wide = jnp.dot(
                scale_ref[d, :, a], spread_r, precision=HIGHEST, preferred_element_type=F32
            )
            h.append(
                jnp.dot(spread_z, wide, precision=HIGHEST, preferred_element_type=F32)
            )
        flat = h[1] * eig_row + h[2] * eig_lane
        for i in range(n):
            total = h[0] * eig_ref[i] + flat
            if scale_out is not None:
                scale_out[a * n + i] = total
            inverse_out[a * n + i] = 1.0 / total


def kernel(
    res_hbm, scale_ref, route_ref, inverse_hbm,
    bf_ref, ef_ref, qf_ref, bm_ref, em_ref, qm_ref, bl_ref, el_ref, pm_ref, plow_ref,
    out_hbm,
    res, first, second, work, scale_f, inv_f, rhs_m, smooth_m, work_m, scale_m, inv_m,
    rhs_l, smooth_l, inv_l, total_l,
    right_f, left_f, right_rf, left_rf, right_pf, left_pf,
    right_m, left_m, right_rm, left_rm, right_l, left_l, right_pp, left_pp,
    dense, target_hot, slot_hot, row_hot, place_hot, sel_hot, vector, partial,
    flat_a, send_a, recv_a, flat_b, send_b, recv_b, cs_plane, cs_row, cr_plane, cr_row,
    hold_f, hold_m, hold_l,
    fs_ax, fr_ax, fs_az, fr_az, fs_dg, fr_dg,
    ms_ax, mr_ax, ms_az, mr_az, ms_dg, mr_dg,
    ls_ax, lr_ax, ls_az, lr_az, ls_dg, lr_dg,
    send_sem, recv_sem, load_sem, all_sem, word_sem, out_sem,
    *, n_axial, n_azim,
):
    devices = n_axial * n_azim
    me_a, me_z = lax.axis_index("axial"), lax.axis_index("azim")
    me = me_a * n_azim + me_z

    def neighbour(da, dz):
        return (lax.rem(me_a + n_axial + da, n_axial), lax.rem(me_z + n_azim + dz, n_azim))

    load_res = pltpu.make_async_copy(res_hbm, res, load_sem.at[0])
    load_res.start()
    load_dense = pltpu.make_async_copy(inverse_hbm.at[0, 0], dense, load_sem.at[1])
    load_dense.start()

    barrier = pltpu.get_barrier_semaphore()

    for j in range(1, n_axial):
        other = (lax.rem(me_a + j, n_axial), me_z)
        pl.semaphore_signal(barrier, inc=1, device_id=other, device_id_type=MESH)
    for j in range(1, n_azim):
        other = (me_a, lax.rem(me_z + j, n_azim))
        pl.semaphore_signal(barrier, inc=1, device_id=other, device_id_type=MESH)
    for da, dz in DIRS[4:]:
        pl.semaphore_signal(barrier, inc=1, device_id=neighbour(da, dz), device_id_type=MESH)

    def spread_word():
        pl.semaphore_wait(barrier, n_axial - 1 + n_azim - 1 + 4)
        for j in range(1, n_azim):
            other = (me_a, lax.rem(me_z + j, n_azim))
            pl.semaphore_signal(word_sem, inc=1, device_id=other, device_id_type=MESH)

    first_device, last_device = me_a == 0, me_a == n_axial - 1
    weight_low_end = jnp.where(first_device, 1.0, 0.5).astype(F32)
    weight_high_end = jnp.where(last_device, 1.0, 0.5).astype(F32)

    faces = {
        8: (fs_ax, fr_ax, fs_az, fr_az, fs_dg, fr_dg),
        4: (ms_ax, mr_ax, ms_az, mr_az, ms_dg, mr_dg),
        2: (ls_ax, lr_ax, ls_az, lr_az, ls_dg, lr_dg),
    }
    pending = []

    def copies_of(e, slot, n):
        s_ax, r_ax, s_az, r_az, s_dg, r_dg = faces[n]
        made = []
        for d, (da, dz) in enumerate(DIRS):
            if d < 2:
                source, target = s_ax.at[slot, d], r_ax.at[slot, d]
            elif d < 4:
                source, target = s_az.at[slot, d - 2], r_az.at[slot, d - 2]
            else:
                source, target = s_dg.at[slot, d - 4], r_dg.at[slot, d - 4]
            made.append(
                pltpu.make_async_remote_copy(
                    src_ref=source, dst_ref=target,
                    send_sem=send_sem.at[e, d], recv_sem=recv_sem.at[e, d],
                    device_id=neighbour(da, dz), device_id_type=MESH,
                )
            )
        return made

    def join_pairs(buf, planes, step):
        if step is not None:
            for at in range(step, buf.shape[1], step):
                both = buf[planes, at - 1 : at, :] + buf[planes, at : at + 1, :]
                buf[planes, at - 1 : at, :] = both
                buf[planes, at : at + 1, :] = both

    def send_ends(e, slot, n, buf, step):
        planes, rows, _ = buf.shape
        join_pairs(buf, slice(0, 1), step)
        join_pairs(buf, slice(planes - 1, planes), step)
        s_ax, s_dg = faces[n][0], faces[n][4]
        s_ax[slot, 0] = buf[planes - 1]
        s_ax[slot, 1] = buf[0]
        s_dg[slot, 0] = buf[planes - 1, rows - 1 : rows]
        s_dg[slot, 1] = buf[planes - 1, 0:1]
        s_dg[slot, 2] = buf[0, rows - 1 : rows]
        s_dg[slot, 3] = buf[0, 0:1]
        made = copies_of(e, slot, n)
        for copy in made[4:] + made[:2]:
            copy.start()
        pending.extend(made)
        return made

    def send_rows(made, slot, n, buf, step, weighted):
        planes, rows, _ = buf.shape
        join_pairs(buf, slice(1, planes - 1), step)
        both = buf[n - 1] + buf[n]
        if weighted:
            both = 0.5 * both
        buf[n - 1] = both
        buf[n] = both
        s_az = faces[n][2]
        for i in range(planes):
            s_az[slot, 0, i : i + 1] = buf[i, rows - 1 : rows]
            s_az[slot, 1, i : i + 1] = buf[i, 0:1]
        for copy in made[2:4]:
            copy.start()

    def send_faces(e, slot, n, buf, step, weighted):
        made = send_ends(e, slot, n, buf, step)
        send_rows(made, slot, n, buf, step, weighted)
        return made

    def join_rows(made, slot, n, buf):
        planes, rows, _ = buf.shape
        r_az = faces[n][3]
        for copy in made[2:4]:
            copy.wait_recv()
        for i in range(planes):
            buf[i, 0:1] = buf[i, 0:1] + r_az[slot, 0, i : i + 1]
            buf[i, rows - 1 : rows] = buf[i, rows - 1 : rows] + r_az[slot, 1, i : i + 1]

    def join_planes(made, slot, n, buf, weighted):
        planes, r_ax = buf.shape[0], faces[n][1]
        for copy in made[:2]:
            copy.wait_recv()
        for end, plane, device, weight in (
            (0, 0, first_device, weight_low_end),
            (1, planes - 1, last_device, weight_high_end),
        ):
            total = buf[plane] + jnp.where(device, 0.0, r_ax[slot, end])
            buf[plane] = total * weight if weighted else total

    def join_faces(made, slot, n, buf, weighted):
        join_rows(made, slot, n, buf)
        join_planes(made, slot, n, buf, weighted)

    def join_corners(made, slot, n, buf, weighted):
        r_dg, hold = faces[n][5], holds[n]
        for copy in made[4:]:
            copy.wait_recv()
        for k in range(4):
            end = k // 2
            line = jnp.where((first_device, last_device)[end], 0.0, r_dg[slot, k])
            if weighted:
                line = line * (weight_low_end, weight_high_end)[end]
            hold[k : k + 1] = line
            if buf is not None:
                plane, row = (0, buf.shape[0] - 1)[end], (0, buf.shape[1] - 1)[k % 2]
                buf[plane, row : row + 1] = buf[plane, row : row + 1] + line
        return hold[...]

    def add_corners(blocks, table, columns, lines):
        half, count = table.shape[0] // 2, len(blocks) // 2
        table = table[:, :128].astype(F32)
        for k, column in enumerate(columns):
            at = (0, count - 1, count, 2 * count - 1)[k]
            factor = table[:half, column : column + 1] + table[half:, column : column + 1]
            blocks[at] = blocks[at] + factor * lines[k : k + 1]
        return blocks

    FINE_CORNERS, MID_CORNERS = (0, 15, 112, 127), (0, 15, 48, 63)
    holds = {8: hold_f, 4: hold_m, 2: hold_l}
    for hold in holds.values():
        hold[...] = jnp.zeros(hold.shape, F32)

    def fine_right(x, which, joined):
        planes, rows, lanes = x.shape
        x = x.reshape(planes * rows, lanes)
        left = wide_right(x[:, :128], right_f[2 * which])
        right = wide_right(x[:, 128:], right_f[2 * which + 1])
        if joined:
            lane = iota(left.shape, 1)
            left, right = (
                left + jnp.where(lane == 127, pltpu.roll(right, 127, 1), 0.0),
                right + jnp.where(lane == 0, pltpu.roll(left, 1, 1), 0.0),
            )
        return jnp.concatenate([left, right], 1).reshape(planes, rows, lanes)

    def fine_left(x, which):
        half = 6
        blocks = cut_rows(x, 8, 16)
        table = left_f[which]
        return wide_left(table, blocks[:half]) + wide_left(table, blocks[half:])

    def fine_pass(source, which, factor, result, e, weighted, came=None, corners=None):
        if came is not None:
            join_rows(*came[:4])
        inner = fine_right(source(1, 15), 2 * which, False)
        if came is not None:
            join_planes(*came)
        ends = jnp.concatenate([source(0, 1), source(15, 16)], 0)
        ends = fine_right(ends, 2 * which, False)
        z = fine_left(jnp.concatenate([ends[0:1], inner, ends[1:2]], 0), 2 * which)
        if corners is not None:
            lines = fine_right(corners().reshape(1, 16, 256), 2 * which, False).reshape(16, 256)
            z = add_corners(z, left_f[2 * which], FINE_CORNERS, lines)
        z = paste_rows(z, 8) * factor[...]
        z = paste_rows(fine_left(z, 2 * which + 1), 8)
        ends = fine_right(jnp.concatenate([z[0:1], z[15:16]], 0), 2 * which + 1, True)
        result[0] = ends[0]
        result[15] = ends[1]
        if e == 0:
            spread_word()
        made = send_ends(e, e, 8, result, 16)
        result[1:15] = fine_right(z[1:15], 2 * which + 1, True)
        send_rows(made, e, 8, result, 16, weighted)
        return made

    basis, basis_t = tables_of(bf_ref)

    def put_fine(at, table, turned, weighted):
        value = right_table(table, 8, 8, 16)
        put_right(right_f, 4 * at, value)
        put_right(right_f, 4 * at + 1, value)
        put_left(left_f, 2 * at, left_table(turned, 8, 8, 2))
        for end in range(2):
            value = right_table(
                turned, 8, 8, 16, joined=True, weighted=weighted, first=end == 0, last=end == 1
            )
            put_right(right_f, 4 * at + 2 + end, value)
        put_left(left_f, 2 * at + 1, left_table(table, 8, 8, 2, joined=True, weighted=weighted))

    put_fine(0, basis, basis_t, True)
    put_scales(scale_ref, ef_ref, 8, scale_f, inv_f)

    load_res.wait()
    made = fine_pass(lambda i, j: res[i:j], 0, inv_f, first, 0, True)

    oper, oper_t = tables_of(qf_ref)
    put_fine(1, oper, oper_t, False)

    came = (made, 0, 8, first, True)
    made = fine_pass(
        lambda i, j: first[i:j], 1, scale_f, work, 1, False, came, lambda: join_corners(*came)
    )

    put_scales(scale_ref, em_ref, 4, scale_m, inv_m)
    pm, pm_t = tables_of(pm_ref, True)
    value = right_table(pm, 4, 8, joined=True, weigh_input=True)
    put_right(right_rf, 0, value[:128])
    put_right(right_rf, 1, value[128:])
    put_left(left_rf, 0, left_table(pm_t, 4, 8, 2, joined=True, weigh_input=True))

    def put_mid(at, table, turned, weighted):
        put_right(right_m, 2 * at, right_table(table, 4, 4))
        put_left_twice(left_m, 2 * at, left_table(turned, 4, 4, 4, copies=2))
        put_right(right_m, 2 * at + 1, right_table(turned, 4, 4, joined=True, weighted=weighted))
        value = left_table(table, 4, 4, 4, joined=True, weighted=weighted, copies=2)
        put_left_twice(left_m, 2 * at + 1, value)

    came_work = (made, 1, 8, work, False)
    made = fine_pass(
        lambda i, j: res[i:j] - work[i:j], 0, inv_f, second, 2, True,
        came_work, lambda: -join_corners(*came_work),
    )

    oper, oper_t = tables_of(qm_ref)
    put_mid(1, oper, oper_t, False)
    put_scales(scale_ref, el_ref, 2, None, inv_l)

    came_second = (made, 2, 8, second, True)

    def joined_first():
        first[...] = first[...] + second[...]
        return join_corners(made, 2, 8, first, True)

    made = fine_pass(
        lambda i, j: first[i:j] + second[i:j], 1, scale_f, work, 3, False,
        came_second, joined_first,
    )

    plow, plow_t = tables_of(plow_ref, True)
    value = right_table(plow, 2, 4, joined=True, weigh_input=True, copies=2)
    high, low = split(value)
    value = jnp.where(iota(value.shape, 1) < 64, high.astype(F32), low.astype(F32)).astype(BF)
    right_rm[0, 0:128] = value
    right_rm[0, 128:256] = value
    value = left_table(plow_t, 2, 4, 4, joined=True, weigh_input=True, copies=2)
    put_left_twice(left_rm, 0, value)
    basis, basis_t = tables_of(bl_ref)
    put_pair(right_l, 0, right_table(basis, 2, 2))
    put_pair(left_l, 0, left_table(basis_t, 2, 2, EZ))
    put_pair(right_l, 1, right_table(basis_t, 2, 2, joined=True, weighted=True))
    put_pair(left_l, 1, left_table(basis, 2, 2, EZ, joined=True, weighted=True))

    join_faces(made, 3, 8, work, False)

    def ends_weighed(x, n):
        planes = x.shape[0]
        return jnp.concatenate(
            [
                x[0:1] * weight_low_end, x[1 : n - 1], x[n - 1 : n + 1] * 0.5,
                x[n + 1 : planes - 1], x[planes - 1 :] * weight_high_end,
            ],
            0,
        )

    blocks = cut_rows(ends_weighed(res[...] - work[...], 8), 8, 16)
    blocks = wide_left(left_rf[0], blocks[:6]) + wide_left(left_rf[0], blocks[6:])
    lines = -join_corners(made, 3, 8, None, True)
    x = paste_rows(add_corners(blocks, left_rf[0], FINE_CORNERS, lines), 4)
    x = x.reshape(384, 256)
    x = wide_right(x[:, :128], right_rf[0]) + wide_right(x[:, 128:], right_rf[1])
    rhs_m[...] = x.reshape(8, 48, 128)
    made = send_faces(4, 0, 4, rhs_m, 8, False)

    route = route_ref[...]
    hot = picked(iota((64, 768), 0) == route)
    target_hot[...] = hot.astype(BF)
    earlier = picked(iota((768, 768), 0) < iota((768, 768), 1)).astype(BF)
    rank = jnp.sum(mm(target_hot[...], earlier) * hot, axis=0, keepdims=True)
    slot_hot[...] = jnp.transpose(picked(iota((128, 768), 0).astype(F32) == rank)).astype(BF)
    half = jnp.where(rank >= HALF_CAP, 1.0, 0.0)
    owner = 2 * route + jnp.where(rank >= HALF_CAP, 1, 0)
    row_hot[...] = picked(iota((128, 768), 0) == owner).astype(BF)
    place_hot[...] = picked(iota((16, 768), 0).astype(F32) == rank - HALF_CAP * half)

    basis, basis_t = tables_of(bm_ref)
    put_mid(0, basis, basis_t, True)
    join_faces(made, 0, 4, rhs_m, False)

    def mid_right(x, at):
        planes, rows, lanes = x.shape
        return wide_right(x.reshape(planes * rows, lanes), right_m[at]).reshape(x.shape)

    def mid_pass(x, which, factor, corners):
        at = 2 * which
        blocks = wide_left(left_m[at], cut_rows(mid_right(x, at), 4, 16))
        lines = mid_right(corners().reshape(1, 16, 128), at).reshape(16, 128)
        x = paste_rows(add_corners(blocks, left_m[at], MID_CORNERS, lines), 4) * factor[...]
        x = mid_right(x, at + 1)
        return paste_rows(wide_left(left_m[at + 1], cut_rows(x, 4, 16)), 4)

    smooth_m[...] = mid_pass(
        rhs_m[...], 0, inv_m, lambda: join_corners(made, 0, 4, rhs_m, False)
    )
    made = send_faces(5, 1, 4, smooth_m, 16, True)
    put_right(right_pf, 0, right_table(pm_t, 8, 4))
    put_left_thrice(left_pf, 0, left_table(pm, 8, 4, 4, copies=3))
    join_faces(made, 1, 4, smooth_m, True)

    work_m[...] = mid_pass(
        smooth_m[...], 1, scale_m, lambda: join_corners(made, 1, 4, smooth_m, True)
    )
    made = send_faces(6, 2, 4, work_m, 16, False)
    both = jnp.zeros((8, 128), F32)
    both_t = jnp.zeros((8, 128), F32)
    for k in range(4):
        both = both + pm[:, k : k + 1] * plow[k : k + 1, :]
        both_t = both_t + plow_t[:, k : k + 1] * pm_t[k : k + 1, :]
    put_pair(right_pp, 0, right_table(both_t, 8, 2))
    put_left_thrice(left_pp, 0, left_table(both, 8, 2, 4, copies=3))
    join_faces(made, 2, 4, work_m, False)

    blocks = cut_rows(ends_weighed(rhs_m[...] - work_m[...], 4), 4, 16)
    blocks = wide_left(left_rm[0], blocks)
    lines = -join_corners(made, 2, 4, None, True)
    x = paste_rows(add_corners(blocks, left_rm[0], MID_CORNERS, lines), 2).reshape(96, 128)
    rhs_l[...] = wide_right(x, right_rm[0]).reshape(4, 24, 64)
    made = send_faces(7, 0, 2, rhs_l, 8, False)

    slot = iota((128, 3072), 0)
    lane = iota((1, 3072), 1)
    half_lane = jnp.where(lane >= 1536, 1, 0)
    rest = lane - 1536 * half_lane
    source = jnp.floor((rest.astype(F32) + 0.5) * (1.0 / HALF_CAP)).astype(jnp.int32)
    wanted = half_lane * HALF_CAP + rest - source * HALF_CAP
    sel_hot[...] = picked(slot == wanted).astype(BF)
    join_faces(made, 0, 2, rhs_l, False)
    join_corners(made, 0, 2, rhs_l, False)

    values = []
    lane = iota((24, 384), 1)
    mine = iota((24, 384), 0) == 2 * (lane >> 5)
    pick_r = picked(iota((64, 384), 0) == 2 * (iota((64, 384), 1) & 31))
    for a in range(2):
        wide = jnp.dot(rhs_l[2 * a], pick_r, precision=HIGHEST, preferred_element_type=F32)
        values.append(jnp.sum(jnp.where(mine, wide, 0.0), axis=0, keepdims=True))
    values = jnp.concatenate(values, 1)
    both = mm(jnp.concatenate(split(target_hot[...].astype(F32) * values), 0), slot_hot[...])
    flat_a[...] = both[:64] + both[64:]
    for t in range(64):
        send_a[t] = flat_a[t : t + 1]

    def spread_out(source, row_of, target, sem):
        def start(a, z):
            pltpu.make_async_remote_copy(
                src_ref=source.at[row_of(a, z)], dst_ref=target.at[me],
                send_sem=all_sem.at[sem], recv_sem=all_sem.at[sem + 1],
                device_id=(a, z), device_id_type=MESH,
            ).start()

        around = [lax.rem(me_z + j, n_azim) for j in range(n_azim)]

        def start_line(j, carry):
            a = lax.rem(me_a + j, n_axial)
            for z in around:
                start(a, z)
            return carry

        lax.fori_loop(1, n_axial, start_line, 0)
        for z in around[1:]:
            start(me_a, z)
        target[me] = source[row_of(me_a, me_z)]

    def wait_all(target, sem):
        some = target.at[pl.ds(0, devices - 1)]
        pltpu.make_async_copy(some, some, all_sem.at[sem]).wait()

    pl.semaphore_wait(word_sem, n_azim - 1)
    spread_out(send_a, lambda a, z: a * (n_azim // 2) + z // 2, recv_a, 0)

    def low_pass(x, factor):
        for side in range(2):
            y = mm_right(x.reshape(96, 64), right_l.at[side]).reshape(2, 48, 64)
            x = jnp.concatenate(
                [mm_left(left_l.at[side], y[a]).reshape(2, 24, 64) for a in range(2)], 0
            )
            if side == 0:
                x = x * factor[...]
        return x

    smooth_l[...] = low_pass(rhs_l[...], inv_l)
    made = send_faces(8, 1, 2, smooth_l, None, True)
    wait_all(recv_a, 1)
    for d in range(devices):
        flat_b[d : d + 1] = recv_a[d]
    wide = mm(jnp.concatenate(split(flat_b[...]), 0), sel_hot[...])
    wide = wide[:devices] + wide[devices:]
    wide = jnp.where(iota((128, 3072), 0) == source, wide, 0.0)
    vector[...] = jnp.broadcast_to(jnp.sum(wide, axis=0, keepdims=True), (8, 3072))
    load_dense.wait()

    def rows_of(r, carry):
        base = pl.multiple_of(r * 32, 32)
        sums = [None] * 4
        for c in range(24):
            v = vector[:, c * 128 : (c + 1) * 128]
            for k in range(4):
                term = dense[pl.ds(base + 8 * k, 8), c * 128 : (c + 1) * 128] * v
                sums[k] = term if sums[k] is None else sums[k] + term
        for k in range(4):
            partial[pl.ds(base + 8 * k, 8), :] = sums[k]
        return carry

    lax.fori_loop(0, 48, rows_of, 0)
    sums = mm(jnp.concatenate(split(partial[...]), 1), jnp.ones((256, 128), BF))
    row = iota((1536, 128), 0)
    group = jnp.floor((row.astype(F32) + 0.5) * (1.0 / HALF_CAP)).astype(jnp.int32)
    sums = jnp.where(iota((1536, 128), 1) == row - group * HALF_CAP, sums, 0.0)
    lane = iota((1, 1536), 1)
    group = jnp.floor((lane.astype(F32) + 0.5) * (1.0 / HALF_CAP)).astype(jnp.int32)
    gather = picked(iota((128, 1536), 0) == group).astype(BF)
    both = mm(gather, jnp.concatenate(split(sums), 1))
    flat_b[...] = both[:, :128] + both[:, 128:]
    for d in range(devices):
        send_b[d] = flat_b[d : d + 1]
    spread_out(send_b, lambda a, z: a * n_azim + z, recv_b, 2)

    x = wide_right(smooth_m[...].reshape(384, 128), right_pf[0]).reshape(8, 48, 256)
    x = paste_rows(thrice_left(left_pf[0], cut_rows(x, 4, 16)), 8)
    second[...] = first[...] + x
    join_faces(made, 1, 2, smooth_l, True)
    join_corners(made, 1, 2, smooth_l, True)

    wait_all(recv_b, 3)
    for d in range(devices):
        flat_b[d : d + 1] = recv_b[d]

    turned = jnp.transpose(flat_b[...])[0:16]
    high, low = split(turned)
    answers = mm(high, row_hot[...]) + mm(low, row_hot[...])
    answers = jnp.sum(answers * place_hot[...], axis=0, keepdims=True)
    row = iota((24, 384), 0)
    belongs = (iota((24, 384), 1) >> 5) == ((row + 1) >> 1)
    to_lanes = picked(
        (iota((384, 64), 0) & 31) == ((iota((384, 64), 1) + 1) >> 1)
    ).astype(BF)
    grids = []
    for a in range(2):
        high, low = split(jnp.where(belongs, answers[:, a * 384 : (a + 1) * 384], 0.0))
        grids.append(mm(high, to_lanes) + mm(low, to_lanes))
    cs_plane[...] = grids[0]
    cs_row[0] = grids[0][0:1]
    cs_row[1] = grids[1][0:1]
    made = []
    for k, (source, target, da, dz) in enumerate((
        (cs_plane, cr_plane, -1, 0),
        (cs_row, cr_row.at[pl.ds(0, 2)], 0, -1),
        (cs_row.at[0], cr_row.at[2], -1, -1),
    )):
        copy = pltpu.make_async_remote_copy(
            src_ref=source, dst_ref=target,
            send_sem=send_sem.at[9, k], recv_sem=recv_sem.at[9, k],
            device_id=neighbour(da, dz), device_id_type=MESH,
        )
        copy.start()
        made.append(copy)
    pending.extend(made)
    for copy in made:
        copy.wait_recv()
    last_row = iota((24, 64), 0) == 23
    lower = jnp.where(last_row, cr_row[0], grids[0])
    upper = jnp.where(last_row, cr_row[1], grids[1])
    beyond = jnp.where(last_device, 0.0, jnp.where(last_row, cr_row[2], cr_plane[...]))
    total_l[0] = smooth_l[0] + lower
    total_l[1] = smooth_l[1] + upper
    total_l[2] = smooth_l[2] + upper
    total_l[3] = smooth_l[3] + beyond

    wide = mm_right(total_l[...].reshape(96, 64), right_pp.at[0]).reshape(4, 24, 256)
    out_copies = []
    for a in range(2):
        z = thrice_left(left_pp[0], cut_rows(wide[2 * a : 2 * a + 2], 2, 8))
        z = jnp.concatenate([b.reshape(8, 32, 256) for b in z], 1)
        part = pl.ds(8 * a, 8)
        second[part] = second[part] + z
        out_copies.append(
            pltpu.make_async_copy(second.at[part], out_hbm.at[part], out_sem.at[a])
        )
        out_copies[a].start()

    for copy in pending:
        copy.wait_send()
    wait_all(recv_a, 0)
    wait_all(recv_b, 2)
    for copy in out_copies:
        copy.wait()


def on_device(
    residual, element_scale, basis_fine, eigen_fine, operator_fine, basis_mid, eigen_mid,
    operator_mid, basis_low, eigen_low, prolong_mid, prolong_low, vertex_route, coarse_inverse,
):
    devices = lax.axis_size("axial") * lax.axis_size("azim")

    def vm(*shape, dtype=F32):
        return pltpu.VMEM(shape, dtype)

    def face_buffers(count, planes, rows, lanes):
        return [
            vm(count, 2, rows, lanes), vm(count, 2, rows, lanes),
            vm(count, 2, planes, lanes), vm(count, 2, planes, lanes),
            vm(count, 4, 1, lanes), vm(count, 4, 1, lanes),
        ]

    fine, mid, low = (16, 96, 256), (8, 48, 128), (4, 24, 64)
    scratch = [
        vm(*fine), vm(*fine), vm(*fine), vm(*fine), vm(*fine), vm(*fine),
        vm(*mid), vm(*mid), vm(*mid), vm(*mid), vm(*mid),
        vm(*low), vm(*low), vm(*low), vm(*low),
        vm(8, 256, 256, dtype=BF), vm(4, 256, 256, dtype=BF),
        vm(2, 256, 256, dtype=BF), vm(1, 64, 256, dtype=BF),
        vm(1, 256, 512, dtype=BF), vm(1, 256, 192, dtype=BF),
        vm(4, 256, 256, dtype=BF), vm(4, 128, 128, dtype=BF),
        vm(1, 256, 128, dtype=BF), vm(1, 32, 128, dtype=BF),
        vm(2, 2, 64, 64, dtype=BF), vm(2, 2, 48, 48, dtype=BF),
        vm(1, 2, 64, 256, dtype=BF), vm(1, 256, 48, dtype=BF),
        vm(1536, 3072), vm(64, 768, dtype=BF), vm(768, 128, dtype=BF), vm(128, 768, dtype=BF),
        vm(16, 768), vm(128, 3072, dtype=BF), vm(8, 3072), vm(1536, 128),
        vm(64, 128), vm(64, 1, 128), vm(devices, 1, 128),
        vm(devices, 128), vm(devices, 1, 128), vm(devices, 1, 128),
        vm(24, 64), vm(2, 1, 64), vm(24, 64), vm(3, 1, 64),
        vm(16, 256), vm(16, 128), vm(16, 64),
        *face_buffers(4, *fine), *face_buffers(3, *mid), *face_buffers(2, *low),
        pltpu.SemaphoreType.DMA((10, 8)), pltpu.SemaphoreType.DMA((10, 8)),
        pltpu.SemaphoreType.DMA((2,)), pltpu.SemaphoreType.DMA((4,)),
        pltpu.SemaphoreType.REGULAR, pltpu.SemaphoreType.DMA((2,)),
    ]
    in_vmem = pl.BlockSpec(memory_space=pltpu.VMEM)
    in_smem = pl.BlockSpec(memory_space=pltpu.SMEM)
    anywhere = pl.BlockSpec(memory_space=pl.ANY)
    call = pl.pallas_call(
        functools.partial(
            kernel, n_axial=lax.axis_size("axial"), n_azim=lax.axis_size("azim")
        ),
        out_shape=jax.ShapeDtypeStruct(residual.shape, F32),
        in_specs=[anywhere, in_vmem, in_vmem, anywhere] + [in_smem] * 10,
        out_specs=anywhere,
        scratch_shapes=scratch,
        compiler_params=pltpu.CompilerParams(
            collective_id=0, has_side_effects=True, vmem_limit_bytes=58 * 1024 * 1024
        ),
        cost_estimate=pl.CostEstimate(
            flops=12_000_000_000, bytes_accessed=24_000_000, transcendentals=0
        ),
    )
    return call(
        residual, jnp.transpose(element_scale, (0, 2, 1, 3)), vertex_route.reshape(1, -1), coarse_inverse,
        basis_fine, eigen_fine, operator_fine, basis_mid, eigen_mid, operator_mid,
        basis_low, eigen_low, prolong_mid.T, prolong_low.T,
    )


def solution(mesh):
    return jax.shard_map(
        on_device,
        mesh=mesh,
        in_specs=(
            P("axial", "azim", None),
            P(None, "axial", "azim", None),
            P(), P(), P(), P(), P(), P(), P(), P(), P(), P(),
            P("axial", "azim", None, None),
            P("axial", "azim", None, None),
        ),
        out_specs=P("axial", "azim", None),
        check_vma=False,
    )
```

```python
import functools

import jax
import jax.numpy as jnp
from jax import lax
from jax.experimental import pallas as pl
from jax.experimental.pallas import tpu as pltpu
from jax.sharding import PartitionSpec as P

F32 = jnp.float32
BF = jnp.bfloat16
HIGHEST = lax.Precision.HIGHEST
MESH = pl.DeviceIdType.MESH

EZ, ER = 12, 32
HALF_CAP = 12
DIRS = ((1, 0), (-1, 0), (0, 1), (0, -1), (1, 1), (1, -1), (-1, 1), (-1, -1))


def iota(shape, dim):
    return lax.broadcasted_iota(jnp.int32, shape, dim)


def split(x):
    high = x.astype(BF)
    return high, (x - high.astype(F32)).astype(BF)


def mm(a, b):
    return jnp.dot(a, b, preferred_element_type=F32)


def mm_right(x, table):
    high, low = split(x)
    return mm(high, table[0]) + mm(high, table[1]) + mm(low, table[0])


def mm_left(table, x):
    high, low = split(x)
    return mm(table[0], high) + mm(table[1], high) + mm(table[0], low)


def wide_right(x, table):
    high, low = split(x)
    both = mm(jnp.concatenate([high, low], 1), table)
    size = table.shape[1] // 2
    return both[:, :size] + both[:, size:]


def wide_left(table, blocks):
    high, low = split(jnp.concatenate(blocks, 1))
    both = mm(table, jnp.concatenate([high, low], 0))
    size = table.shape[0] // 2
    both = both[:size] + both[size:]
    lanes = blocks[0].shape[1]
    return [both[:, k * lanes : (k + 1) * lanes] for k in range(len(blocks))]


def thrice_left(table, blocks):
    high, low = split(jnp.concatenate(blocks, 1))
    both = mm(table, jnp.concatenate([high, high, low], 0))
    lanes = blocks[0].shape[1]
    return [both[:, k * lanes : (k + 1) * lanes] for k in range(len(blocks))]


def cut_rows(x, n, rows):
    planes, length, lanes = x.shape
    return [
        x[a * n : a * n + n, r : r + rows].reshape(n * rows, lanes)
        for a in range(planes // n)
        for r in range(0, length, rows)
    ]


def paste_rows(blocks, n):
    rows, lanes = blocks[0].shape[0] // n, blocks[0].shape[1]
    half = len(blocks) // 2
    blocks = [b.reshape(n, rows, lanes) for b in blocks]
    return jnp.concatenate(
        [jnp.concatenate(blocks[:half], 1), jnp.concatenate(blocks[half:], 1)], 0
    )


def picked(condition):
    return jnp.where(condition, 1.0, 0.0).astype(F32)


def quotient(x, size, count):
    if size & (size - 1) == 0:
        return x >> (size.bit_length() - 1)
    total = jnp.zeros_like(x)
    for k in range(1, count):
        total = total + jnp.where(x >= size * k, 1, 0)
    return total


def tables_of(ref, turned_in=False):
    n, m = ref.shape if turned_in else ref.shape[::-1]
    row, lane = iota((8, 128), 0), iota((8, 128), 1)
    plain = jnp.where(lane < 8, row * 8 + lane, -1)
    turned = jnp.where(lane < 8, lane * 8 + row, -1)
    table = jnp.zeros((8, 128), F32)
    transposed = jnp.zeros((8, 128), F32)
    for i in range(m):
        for j in range(n):
            value = ref[j, i] if turned_in else ref[i, j]
            table = jnp.where(plain == i * 8 + j, value, table)
            transposed = jnp.where(turned == i * 8 + j, value, transposed)
    return table, transposed


def spread_columns(table, count, length, place):
    index = place(iota((8, length), 1))
    result = jnp.zeros((8, length), F32)
    for j in range(count):
        result = jnp.where(index == j, table[:, j : j + 1], result)
    return result


def spread_rows(table, length, place):
    high = table.astype(BF).astype(F32)
    rest = table - high
    middle = rest.astype(BF).astype(F32)
    pieces = jnp.concatenate([high, middle, rest - middle], 0).astype(BF)
    index = place(iota((length, 24), 0))
    return mm(picked((iota((length, 24), 1) & 7) == index).astype(BF), pieces)


def left_table(table, m, n, group, joined=False, weighted=False, weigh_input=False, copies=1):
    rows, columns = m * group * m, n * group * n

    def once(x):
        return x if copies == 1 else x - columns * quotient(x, columns, copies)

    def parts(x, nodes):
        outer = quotient(x, group * nodes, nodes)
        inner = x - outer * (group * nodes)
        block = quotient(inner, nodes, group)
        return outer, block, inner - block * nodes

    first = spread_columns(table, n, copies * columns, lambda x: parts(once(x), n)[0])
    second = spread_columns(table, n, copies * columns, lambda x: parts(once(x), n)[2])
    outer = spread_rows(first, rows, lambda x: parts(x, m)[0])
    inner = spread_rows(second, rows, lambda x: parts(x, m)[2])
    shape = (rows, copies * columns)
    _, row_block, q = parts(iota(shape, 0), m)
    _, column_block, j = parts(once(iota(shape, 1)), n)
    value = jnp.where(row_block == column_block, inner, 0.0)
    if joined:
        value = value + jnp.where(
            (q == m - 1) & (row_block + 1 == column_block), second[0:1], 0.0
        )
        value = value + jnp.where(
            (q == 0) & (row_block - 1 == column_block), second[m - 1 : m], 0.0
        )
    if weighted:
        value = jnp.where((q == 0) | (q == m - 1), 0.5 * value, value)
    if weigh_input:
        value = jnp.where((j == 0) | (j == n - 1), 0.5 * value, value)
    return outer * value


def right_table(
    turned, m, n, count=ER, joined=False, weighted=False, weigh_input=False,
    first=True, last=True, copies=1,
):
    rows, columns = count * n, count * m
    spread = spread_columns(turned, m, copies * columns, lambda x: x & (m - 1))
    inner = spread_rows(spread, rows, lambda x: x & (n - 1))
    shape = (rows, copies * columns)
    row, column = iota(shape, 0), iota(shape, 1) & (columns - 1)
    row_block, k = quotient(row, n, count), row & (n - 1)
    column_block, s = quotient(column, m, count), column & (m - 1)
    value = jnp.where(row_block == column_block, inner, 0.0)
    if joined:
        value = value + jnp.where(
            (s == m - 1) & (column_block + 1 == row_block), inner[:, 0:1], 0.0
        )
        value = value + jnp.where(
            (s == 0) & (column_block - 1 == row_block), inner[:, m - 1 : m], 0.0
        )

    def halved(place, block, nodes, value):
        low, high = place == 0, place == nodes - 1
        if first:
            low = low & (block > 0)
        if last:
            high = high & (block < count - 1)
        return jnp.where(low | high, 0.5 * value, value)

    if weighted:
        value = halved(s, column_block, m, value)
    if weigh_input:
        value = halved(k, row_block, n, value)
    return value


def put_pair(ref, index, value):
    high, low = split(value)
    ref[index, 0] = high
    ref[index, 1] = low


def put_right(ref, index, value):
    rows, columns = value.shape
    high, low = split(value)
    for k in range(2):
        ref[index, k * rows : (k + 1) * rows, 0:columns] = high
        ref[index, k * rows : (k + 1) * rows, columns : 2 * columns] = low


def put_left(ref, index, value):
    rows, columns = value.shape
    high, low = split(value)
    for k in range(2):
        ref[index, 0:rows, k * columns : (k + 1) * columns] = high
        ref[index, rows : 2 * rows, k * columns : (k + 1) * columns] = low


def put_left_twice(ref, index, value):
    rows = value.shape[0]
    high, low = split(value)
    ref[index, 0:rows] = high
    ref[index, rows : 2 * rows] = low


def put_left_thrice(ref, index, value):
    columns = value.shape[1] // 3
    high, low = split(value)
    lane = iota(value.shape, 1)
    middle = (lane >= columns) & (lane < 2 * columns)
    ref[index] = jnp.where(middle, low.astype(F32), high.astype(F32)).astype(BF)


def put_scales(scale_ref, eig_ref, n, scale_out, inverse_out):
    rows, lanes = EZ * n, ER * n
    spread_z = picked(quotient(iota((rows, EZ), 0), n, EZ) == iota((rows, EZ), 1))
    spread_r = picked(iota((ER, lanes), 0) == quotient(iota((ER, lanes), 1), n, ER))
    row = iota((rows, lanes), 0) & (n - 1)
    lane = iota((rows, lanes), 1) & (n - 1)
    eig_row = jnp.zeros((rows, lanes), F32)
    eig_lane = jnp.zeros((rows, lanes), F32)
    for k in range(n):
        eig_row = jnp.where(row == k, eig_ref[k], eig_row)
        eig_lane = jnp.where(lane == k, eig_ref[k], eig_lane)
    for a in range(2):
        h = []
        for d in range(3):
            wide = jnp.dot(
                scale_ref[d, :, a], spread_r, precision=HIGHEST, preferred_element_type=F32
            )
            h.append(
                jnp.dot(spread_z, wide, precision=HIGHEST, preferred_element_type=F32)
            )
        flat = h[1] * eig_row + h[2] * eig_lane
        for i in range(n):
            total = h[0] * eig_ref[i] + flat
            if scale_out is not None:
                scale_out[a * n + i] = total
            inverse_out[a * n + i] = 1.0 / total


def kernel(
    res_hbm, scale_ref, route_ref, inverse_hbm,
    bf_ref, ef_ref, qf_ref, bm_ref, em_ref, qm_ref, bl_ref, el_ref, pm_ref, plow_ref,
    out_hbm,
    res, first, second, work, scale_f, inv_f, rhs_m, smooth_m, work_m, scale_m, inv_m,
    rhs_l, smooth_l, inv_l, total_l,
    right_f, left_f, right_rf, left_rf, right_pf, left_pf,
    right_m, left_m, right_rm, left_rm, right_l, left_l, right_pp, left_pp,
    dense, target_hot, slot_hot, row_hot, place_hot, sel_hot, vector, partial,
    flat_a, send_a, recv_a, flat_b, send_b, recv_b, cs_plane, cs_row, cr_plane, cr_row,
    hold_f, hold_m, hold_l,
    fs_ax, fr_ax, fs_az, fr_az, fs_dg, fr_dg,
    ms_ax, mr_ax, ms_az, mr_az, ms_dg, mr_dg,
    ls_ax, lr_ax, ls_az, lr_az, ls_dg, lr_dg,
    send_sem, recv_sem, load_sem, all_sem, word_sem, out_sem,
    *, n_axial, n_azim,
):
    devices = n_axial * n_azim
    me_a, me_z = lax.axis_index("axial"), lax.axis_index("azim")
    me = me_a * n_azim + me_z

    def neighbour(da, dz):
        return (lax.rem(me_a + n_axial + da, n_axial), lax.rem(me_z + n_azim + dz, n_azim))

    load_res = pltpu.make_async_copy(res_hbm, res, load_sem.at[0])
    load_res.start()
    load_dense = pltpu.make_async_copy(inverse_hbm.at[0, 0], dense, load_sem.at[1])
    load_dense.start()

    barrier = pltpu.get_barrier_semaphore()

    for j in range(1, n_axial):
        other = (lax.rem(me_a + j, n_axial), me_z)
        pl.semaphore_signal(barrier, inc=1, device_id=other, device_id_type=MESH)
    for j in range(1, n_azim):
        other = (me_a, lax.rem(me_z + j, n_azim))
        pl.semaphore_signal(barrier, inc=1, device_id=other, device_id_type=MESH)
    for da, dz in DIRS[4:]:
        pl.semaphore_signal(barrier, inc=1, device_id=neighbour(da, dz), device_id_type=MESH)

    def spread_word():
        pl.semaphore_wait(barrier, n_axial - 1 + n_azim - 1 + 4)
        for j in range(1, n_azim):
            other = (me_a, lax.rem(me_z + j, n_azim))
            pl.semaphore_signal(word_sem, inc=1, device_id=other, device_id_type=MESH)

    first_device, last_device = me_a == 0, me_a == n_axial - 1
    weight_low_end = jnp.where(first_device, 1.0, 0.5).astype(F32)
    weight_high_end = jnp.where(last_device, 1.0, 0.5).astype(F32)

    faces = {
        8: (fs_ax, fr_ax, fs_az, fr_az, fs_dg, fr_dg),
        4: (ms_ax, mr_ax, ms_az, mr_az, ms_dg, mr_dg),
        2: (ls_ax, lr_ax, ls_az, lr_az, ls_dg, lr_dg),
    }
    pending = []

    def copies_of(e, slot, n):
        s_ax, r_ax, s_az, r_az, s_dg, r_dg = faces[n]
        made = []
        for d, (da, dz) in enumerate(DIRS):
            if d < 2:
                source, target = s_ax.at[slot, d], r_ax.at[slot, d]
            elif d < 4:
                source, target = s_az.at[slot, d - 2], r_az.at[slot, d - 2]
            else:
                source, target = s_dg.at[slot, d - 4], r_dg.at[slot, d - 4]
            made.append(
                pltpu.make_async_remote_copy(
                    src_ref=source, dst_ref=target,
                    send_sem=send_sem.at[e, d], recv_sem=recv_sem.at[e, d],
                    device_id=neighbour(da, dz), device_id_type=MESH,
                )
            )
        return made

    def join_pairs(buf, planes, step):
        if step is not None:
            for at in range(step, buf.shape[1], step):
                both = buf[planes, at - 1 : at, :] + buf[planes, at : at + 1, :]
                buf[planes, at - 1 : at, :] = both
                buf[planes, at : at + 1, :] = both

    def send_ends(e, slot, n, buf, step):
        planes, rows, _ = buf.shape
        join_pairs(buf, slice(0, 1), step)
        join_pairs(buf, slice(planes - 1, planes), step)
        s_ax, s_dg = faces[n][0], faces[n][4]
        s_ax[slot, 0] = buf[planes - 1]
        s_ax[slot, 1] = buf[0]
        s_dg[slot, 0] = buf[planes - 1, rows - 1 : rows]
        s_dg[slot, 1] = buf[planes - 1, 0:1]
        s_dg[slot, 2] = buf[0, rows - 1 : rows]
        s_dg[slot, 3] = buf[0, 0:1]
        made = copies_of(e, slot, n)
        for copy in made[4:] + made[:2]:
            copy.start()
        pending.extend(made)
        return made

    def send_rows(made, slot, n, buf, step, weighted):
        planes, rows, _ = buf.shape
        join_pairs(buf, slice(1, planes - 1), step)
        both = buf[n - 1] + buf[n]
        if weighted:
            both = 0.5 * both
        buf[n - 1] = both
        buf[n] = both
        s_az = faces[n][2]
        for i in range(planes):
            s_az[slot, 0, i : i + 1] = buf[i, rows - 1 : rows]
            s_az[slot, 1, i : i + 1] = buf[i, 0:1]
        for copy in made[2:4]:
            copy.start()

    def send_faces(e, slot, n, buf, step, weighted):
        made = send_ends(e, slot, n, buf, step)
        send_rows(made, slot, n, buf, step, weighted)
        return made

    def join_rows(made, slot, n, buf):
        planes, rows, _ = buf.shape
        r_az = faces[n][3]
        for copy in made[2:4]:
            copy.wait_recv()
        for i in range(planes):
            buf[i, 0:1] = buf[i, 0:1] + r_az[slot, 0, i : i + 1]
            buf[i, rows - 1 : rows] = buf[i, rows - 1 : rows] + r_az[slot, 1, i : i + 1]

    def join_planes(made, slot, n, buf, weighted):
        planes, r_ax = buf.shape[0], faces[n][1]
        for copy in made[:2]:
            copy.wait_recv()
        for end, plane, device, weight in (
            (0, 0, first_device, weight_low_end),
            (1, planes - 1, last_device, weight_high_end),
        ):
            total = buf[plane] + jnp.where(device, 0.0, r_ax[slot, end])
            buf[plane] = total * weight if weighted else total

    def join_faces(made, slot, n, buf, weighted):
        join_rows(made, slot, n, buf)
        join_planes(made, slot, n, buf, weighted)

    def join_corners(made, slot, n, buf, weighted):
        r_dg, hold = faces[n][5], holds[n]
        for copy in made[4:]:
            copy.wait_recv()
        for k in range(4):
            end = k // 2
            line = jnp.where((first_device, last_device)[end], 0.0, r_dg[slot, k])
            if weighted:
                line = line * (weight_low_end, weight_high_end)[end]
            hold[k : k + 1] = line
            if buf is not None:
                plane, row = (0, buf.shape[0] - 1)[end], (0, buf.shape[1] - 1)[k % 2]
                buf[plane, row : row + 1] = buf[plane, row : row + 1] + line
        return hold[...]

    def add_corners(blocks, table, columns, lines):
        half, count = table.shape[0] // 2, len(blocks) // 2
        table = table[:, :128].astype(F32)
        for k, column in enumerate(columns):
            at = (0, count - 1, count, 2 * count - 1)[k]
            factor = table[:half, column : column + 1] + table[half:, column : column + 1]
            blocks[at] = blocks[at] + factor * lines[k : k + 1]
        return blocks

    FINE_CORNERS, MID_CORNERS = (0, 15, 112, 127), (0, 15, 48, 63)
    holds = {8: hold_f, 4: hold_m, 2: hold_l}
    for hold in holds.values():
        hold[...] = jnp.zeros(hold.shape, F32)

    def fine_right(x, which, joined):
        planes, rows, lanes = x.shape
        x = x.reshape(planes * rows, lanes)
        left = wide_right(x[:, :128], right_f[2 * which])
        right = wide_right(x[:, 128:], right_f[2 * which + 1])
        if joined:
            lane = iota(left.shape, 1)
            left, right = (
                left + jnp.where(lane == 127, pltpu.roll(right, 127, 1), 0.0),
                right + jnp.where(lane == 0, pltpu.roll(left, 1, 1), 0.0),
            )
        return jnp.concatenate([left, right], 1).reshape(planes, rows, lanes)

    def fine_left(x, which):
        half = 6
        blocks = cut_rows(x, 8, 16)
        table = left_f[which]
        return wide_left(table, blocks[:half]) + wide_left(table, blocks[half:])

    def fine_pass(source, which, factor, result, e, weighted, came=None, corners=None):
        if came is not None:
            join_rows(*came[:4])
        inner = fine_right(source(1, 15), 2 * which, False)
        if came is not None:
            join_planes(*came)
        ends = jnp.concatenate([source(0, 1), source(15, 16)], 0)
        ends = fine_right(ends, 2 * which, False)
        z = fine_left(jnp.concatenate([ends[0:1], inner, ends[1:2]], 0), 2 * which)
        if corners is not None:
            lines = fine_right(corners().reshape(1, 16, 256), 2 * which, False).reshape(16, 256)
            z = add_corners(z, left_f[2 * which], FINE_CORNERS, lines)
        z = paste_rows(z, 8) * factor[...]
        z = paste_rows(fine_left(z, 2 * which + 1), 8)
        ends = fine_right(jnp.concatenate([z[0:1], z[15:16]], 0), 2 * which + 1, True)
        result[0] = ends[0]
        result[15] = ends[1]
        if e == 0:
            spread_word()
        made = send_ends(e, e, 8, result, 16)
        result[1:15] = fine_right(z[1:15], 2 * which + 1, True)
        send_rows(made, e, 8, result, 16, weighted)
        return made

    basis, basis_t = tables_of(bf_ref)

    def put_fine(at, table, turned, weighted):
        value = right_table(table, 8, 8, 16)
        put_right(right_f, 4 * at, value)
        put_right(right_f, 4 * at + 1, value)
        put_left(left_f, 2 * at, left_table(turned, 8, 8, 2))
        for end in range(2):
            value = right_table(
                turned, 8, 8, 16, joined=True, weighted=weighted, first=end == 0, last=end == 1
            )
            put_right(right_f, 4 * at + 2 + end, value)
        put_left(left_f, 2 * at + 1, left_table(table, 8, 8, 2, joined=True, weighted=weighted))

    put_fine(0, basis, basis_t, True)
    put_scales(scale_ref, ef_ref, 8, scale_f, inv_f)

    load_res.wait()
    made = fine_pass(lambda i, j: res[i:j], 0, inv_f, first, 0, True)

    oper, oper_t = tables_of(qf_ref)
    put_fine(1, oper, oper_t, False)

    came = (made, 0, 8, first, True)
    made = fine_pass(
        lambda i, j: first[i:j], 1, scale_f, work, 1, False, came, lambda: join_corners(*came)
    )

    put_scales(scale_ref, em_ref, 4, scale_m, inv_m)
    pm, pm_t = tables_of(pm_ref, True)
    value = right_table(pm, 4, 8, joined=True, weigh_input=True)
    put_right(right_rf, 0, value[:128])
    put_right(right_rf, 1, value[128:])
    put_left(left_rf, 0, left_table(pm_t, 4, 8, 2, joined=True, weigh_input=True))

    def put_mid(at, table, turned, weighted):
        put_right(right_m, 2 * at, right_table(table, 4, 4))
        put_left_twice(left_m, 2 * at, left_table(turned, 4, 4, 4, copies=2))
        put_right(right_m, 2 * at + 1, right_table(turned, 4, 4, joined=True, weighted=weighted))
        value = left_table(table, 4, 4, 4, joined=True, weighted=weighted, copies=2)
        put_left_twice(left_m, 2 * at + 1, value)

    came_work = (made, 1, 8, work, False)
    made = fine_pass(
        lambda i, j: res[i:j] - work[i:j], 0, inv_f, second, 2, True,
        came_work, lambda: -join_corners(*came_work),
    )

    oper, oper_t = tables_of(qm_ref)
    put_mid(1, oper, oper_t, False)
    put_scales(scale_ref, el_ref, 2, None, inv_l)

    came_second = (made, 2, 8, second, True)

    def joined_first():
        first[...] = first[...] + second[...]
        return join_corners(made, 2, 8, first, True)

    made = fine_pass(
        lambda i, j: first[i:j] + second[i:j], 1, scale_f, work, 3, False,
        came_second, joined_first,
    )

    plow, plow_t = tables_of(plow_ref, True)
    value = right_table(plow, 2, 4, joined=True, weigh_input=True, copies=2)
    high, low = split(value)
    value = jnp.where(iota(value.shape, 1) < 64, high.astype(F32), low.astype(F32)).astype(BF)
    right_rm[0, 0:128] = value
    right_rm[0, 128:256] = value
    value = left_table(plow_t, 2, 4, 4, joined=True, weigh_input=True, copies=2)
    put_left_twice(left_rm, 0, value)
    basis, basis_t = tables_of(bl_ref)
    put_pair(right_l, 0, right_table(basis, 2, 2))
    put_pair(left_l, 0, left_table(basis_t, 2, 2, EZ))
    put_pair(right_l, 1, right_table(basis_t, 2, 2, joined=True, weighted=True))
    put_pair(left_l, 1, left_table(basis, 2, 2, EZ, joined=True, weighted=True))

    join_faces(made, 3, 8, work, False)

    def ends_weighed(x, n):
        planes = x.shape[0]
        return jnp.concatenate(
            [
                x[0:1] * weight_low_end, x[1 : n - 1], x[n - 1 : n + 1] * 0.5,
                x[n + 1 : planes - 1], x[planes - 1 :] * weight_high_end,
            ],
            0,
        )

    blocks = cut_rows(ends_weighed(res[...] - work[...], 8), 8, 16)
    blocks = wide_left(left_rf[0], blocks[:6]) + wide_left(left_rf[0], blocks[6:])
    lines = -join_corners(made, 3, 8, None, True)
    x = paste_rows(add_corners(blocks, left_rf[0], FINE_CORNERS, lines), 4)
    x = x.reshape(384, 256)
    x = wide_right(x[:, :128], right_rf[0]) + wide_right(x[:, 128:], right_rf[1])
    rhs_m[...] = x.reshape(8, 48, 128)
    made = send_faces(4, 0, 4, rhs_m, 8, False)

    route = route_ref[...]
    hot = picked(iota((64, 768), 0) == route)
    target_hot[...] = hot.astype(BF)
    earlier = picked(iota((768, 768), 0) < iota((768, 768), 1)).astype(BF)
    rank = jnp.sum(mm(target_hot[...], earlier) * hot, axis=0, keepdims=True)
    slot_hot[...] = jnp.transpose(picked(iota((128, 768), 0).astype(F32) == rank)).astype(BF)
    half = jnp.where(rank >= HALF_CAP, 1.0, 0.0)
    owner = 2 * route + jnp.where(rank >= HALF_CAP, 1, 0)
    row_hot[...] = picked(iota((128, 768), 0) == owner).astype(BF)
    place_hot[...] = picked(iota((16, 768), 0).astype(F32) == rank - HALF_CAP * half)

    basis, basis_t = tables_of(bm_ref)
    put_mid(0, basis, basis_t, True)
    join_faces(made, 0, 4, rhs_m, False)

    def mid_right(x, at):
        planes, rows, lanes = x.shape
        return wide_right(x.reshape(planes * rows, lanes), right_m[at]).reshape(x.shape)

    def mid_pass(x, which, factor, corners):
        at = 2 * which
        blocks = wide_left(left_m[at], cut_rows(mid_right(x, at), 4, 16))
        lines = mid_right(corners().reshape(1, 16, 128), at).reshape(16, 128)
        x = paste_rows(add_corners(blocks, left_m[at], MID_CORNERS, lines), 4) * factor[...]
        x = mid_right(x, at + 1)
        return paste_rows(wide_left(left_m[at + 1], cut_rows(x, 4, 16)), 4)

    smooth_m[...] = mid_pass(
        rhs_m[...], 0, inv_m, lambda: join_corners(made, 0, 4, rhs_m, False)
    )
    made = send_faces(5, 1, 4, smooth_m, 16, True)
    put_right(right_pf, 0, right_table(pm_t, 8, 4))
    put_left_thrice(left_pf, 0, left_table(pm, 8, 4, 4, copies=3))
    join_faces(made, 1, 4, smooth_m, True)

    work_m[...] = mid_pass(
        smooth_m[...], 1, scale_m, lambda: join_corners(made, 1, 4, smooth_m, True)
    )
    made = send_faces(6, 2, 4, work_m, 16, False)
    both = jnp.zeros((8, 128), F32)
    both_t = jnp.zeros((8, 128), F32)
    for k in range(4):
        both = both + pm[:, k : k + 1] * plow[k : k + 1, :]
        both_t = both_t + plow_t[:, k : k + 1] * pm_t[k : k + 1, :]
    put_pair(right_pp, 0, right_table(both_t, 8, 2))
    put_left_thrice(left_pp, 0, left_table(both, 8, 2, 4, copies=3))
    join_faces(made, 2, 4, work_m, False)

    blocks = cut_rows(ends_weighed(rhs_m[...] - work_m[...], 4), 4, 16)
    blocks = wide_left(left_rm[0], blocks)
    lines = -join_corners(made, 2, 4, None, True)
    x = paste_rows(add_corners(blocks, left_rm[0], MID_CORNERS, lines), 2).reshape(96, 128)
    rhs_l[...] = wide_right(x, right_rm[0]).reshape(4, 24, 64)
    made = send_faces(7, 0, 2, rhs_l, 8, False)

    slot = iota((128, 3072), 0)
    lane = iota((1, 3072), 1)
    half_lane = jnp.where(lane >= 1536, 1, 0)
    rest = lane - 1536 * half_lane
    source = jnp.floor((rest.astype(F32) + 0.5) * (1.0 / HALF_CAP)).astype(jnp.int32)
    wanted = half_lane * HALF_CAP + rest - source * HALF_CAP
    sel_hot[...] = picked(slot == wanted).astype(BF)
    join_faces(made, 0, 2, rhs_l, False)
    join_corners(made, 0, 2, rhs_l, False)

    values = []
    lane = iota((24, 384), 1)
    mine = iota((24, 384), 0) == 2 * (lane >> 5)
    pick_r = picked(iota((64, 384), 0) == 2 * (iota((64, 384), 1) & 31))
    for a in range(2):
        wide = jnp.dot(rhs_l[2 * a], pick_r, precision=HIGHEST, preferred_element_type=F32)
        values.append(jnp.sum(jnp.where(mine, wide, 0.0), axis=0, keepdims=True))
    values = jnp.concatenate(values, 1)
    both = mm(jnp.concatenate(split(target_hot[...].astype(F32) * values), 0), slot_hot[...])
    flat_a[...] = both[:64] + both[64:]
    for t in range(64):
        send_a[t] = flat_a[t : t + 1]

    def spread_out(source, row_of, target, sem):
        def start(a, z):
            pltpu.make_async_remote_copy(
                src_ref=source.at[row_of(a, z)], dst_ref=target.at[me],
                send_sem=all_sem.at[sem], recv_sem=all_sem.at[sem + 1],
                device_id=(a, z), device_id_type=MESH,
            ).start()

        around = [lax.rem(me_z + j, n_azim) for j in range(n_azim)]

        def start_line(j, carry):
            a = lax.rem(me_a + j, n_axial)
            for z in around:
                start(a, z)
            return carry

        lax.fori_loop(1, n_axial, start_line, 0)
        for z in around[1:]:
            start(me_a, z)
        target[me] = source[row_of(me_a, me_z)]

    def wait_all(target, sem):
        some = target.at[pl.ds(0, devices - 1)]
        pltpu.make_async_copy(some, some, all_sem.at[sem]).wait()

    pl.semaphore_wait(word_sem, n_azim - 1)
    spread_out(send_a, lambda a, z: a * (n_azim // 2) + z // 2, recv_a, 0)

    def low_pass(x, factor):
        for side in range(2):
            y = mm_right(x.reshape(96, 64), right_l.at[side]).reshape(2, 48, 64)
            x = jnp.concatenate(
                [mm_left(left_l.at[side], y[a]).reshape(2, 24, 64) for a in range(2)], 0
            )
            if side == 0:
                x = x * factor[...]
        return x

    smooth_l[...] = low_pass(rhs_l[...], inv_l)
    made = send_faces(8, 1, 2, smooth_l, None, True)
    wait_all(recv_a, 1)
    for d in range(devices):
        flat_b[d : d + 1] = recv_a[d]
    wide = mm(jnp.concatenate(split(flat_b[...]), 0), sel_hot[...])
    wide = wide[:devices] + wide[devices:]
    wide = jnp.where(iota((128, 3072), 0) == source, wide, 0.0)
    vector[...] = jnp.broadcast_to(jnp.sum(wide, axis=0, keepdims=True), (8, 3072))
    load_dense.wait()

    def rows_of(r, carry):
        base = pl.multiple_of(r * 32, 32)
        sums = [None] * 4
        for c in range(24):
            v = vector[:, c * 128 : (c + 1) * 128]
            for k in range(4):
                term = dense[pl.ds(base + 8 * k, 8), c * 128 : (c + 1) * 128] * v
                sums[k] = term if sums[k] is None else sums[k] + term
        for k in range(4):
            partial[pl.ds(base + 8 * k, 8), :] = sums[k]
        return carry

    lax.fori_loop(0, 48, rows_of, 0)
    sums = mm(jnp.concatenate(split(partial[...]), 1), jnp.ones((256, 128), BF))
    row = iota((1536, 128), 0)
    group = jnp.floor((row.astype(F32) + 0.5) * (1.0 / HALF_CAP)).astype(jnp.int32)
    sums = jnp.where(iota((1536, 128), 1) == row - group * HALF_CAP, sums, 0.0)
    lane = iota((1, 1536), 1)
    group = jnp.floor((lane.astype(F32) + 0.5) * (1.0 / HALF_CAP)).astype(jnp.int32)
    gather = picked(iota((128, 1536), 0) == group).astype(BF)
    both = mm(gather, jnp.concatenate(split(sums), 1))
    flat_b[...] = both[:, :128] + both[:, 128:]
    for d in range(devices):
        send_b[d] = flat_b[d : d + 1]
    spread_out(send_b, lambda a, z: a * n_azim + z, recv_b, 2)

    x = wide_right(smooth_m[...].reshape(384, 128), right_pf[0]).reshape(8, 48, 256)
    x = paste_rows(thrice_left(left_pf[0], cut_rows(x, 4, 16)), 8)
    second[...] = first[...] + x
    join_faces(made, 1, 2, smooth_l, True)
    join_corners(made, 1, 2, smooth_l, True)

    wait_all(recv_b, 3)
    for d in range(devices):
        flat_b[d : d + 1] = recv_b[d]

    turned = jnp.transpose(flat_b[...])[0:16]
    high, low = split(turned)
    answers = mm(high, row_hot[...]) + mm(low, row_hot[...])
    answers = jnp.sum(answers * place_hot[...], axis=0, keepdims=True)
    row = iota((24, 384), 0)
    belongs = (iota((24, 384), 1) >> 5) == ((row + 1) >> 1)
    to_lanes = picked(
        (iota((384, 64), 0) & 31) == ((iota((384, 64), 1) + 1) >> 1)
    ).astype(BF)
    grids = []
    for a in range(2):
        high, low = split(jnp.where(belongs, answers[:, a * 384 : (a + 1) * 384], 0.0))
        grids.append(mm(high, to_lanes) + mm(low, to_lanes))
    cs_plane[...] = grids[0]
    cs_row[0] = grids[0][0:1]
    cs_row[1] = grids[1][0:1]
    made = []
    for k, (source, target, da, dz) in enumerate((
        (cs_plane, cr_plane, -1, 0),
        (cs_row, cr_row.at[pl.ds(0, 2)], 0, -1),
        (cs_row.at[0], cr_row.at[2], -1, -1),
    )):
        copy = pltpu.make_async_remote_copy(
            src_ref=source, dst_ref=target,
            send_sem=send_sem.at[9, k], recv_sem=recv_sem.at[9, k],
            device_id=neighbour(da, dz), device_id_type=MESH,
        )
        made.append(copy)
    pending.extend(made)
    for k in (2, 0, 1):
        made[k].start()
    last_row = iota((24, 64), 0) == 23
    out_copies = []
    for a in range(2):
        if a == 0:
            made[1].wait_recv()
            near = jnp.where(last_row, cr_row[0], grids[0])
            far = jnp.where(last_row, cr_row[1], grids[1])
        else:
            made[0].wait_recv()
            made[2].wait_recv()
            near = far
            beyond = jnp.where(last_row, cr_row[2], cr_plane[...])
            far = jnp.where(last_device, 0.0, beyond)
        total_l[2 * a] = smooth_l[2 * a] + near
        total_l[2 * a + 1] = smooth_l[2 * a + 1] + far
        low = total_l[2 * a : 2 * a + 2].reshape(48, 64)
        wide = mm_right(low, right_pp.at[0]).reshape(2, 24, 256)
        z = thrice_left(left_pp[0], cut_rows(wide, 2, 8))
        z = jnp.concatenate([b.reshape(8, 32, 256) for b in z], 1)
        part = pl.ds(8 * a, 8)
        second[part] = second[part] + z
        out_copies.append(
            pltpu.make_async_copy(second.at[part], out_hbm.at[part], out_sem.at[a])
        )
        out_copies[a].start()

    for copy in pending:
        copy.wait_send()
    wait_all(recv_a, 0)
    wait_all(recv_b, 2)
    for copy in out_copies:
        copy.wait()


def on_device(
    residual, element_scale, basis_fine, eigen_fine, operator_fine, basis_mid, eigen_mid,
    operator_mid, basis_low, eigen_low, prolong_mid, prolong_low, vertex_route, coarse_inverse,
):
    devices = lax.axis_size("axial") * lax.axis_size("azim")

    def vm(*shape, dtype=F32):
        return pltpu.VMEM(shape, dtype)

    def face_buffers(count, planes, rows, lanes):
        return [
            vm(count, 2, rows, lanes), vm(count, 2, rows, lanes),
            vm(count, 2, planes, lanes), vm(count, 2, planes, lanes),
            vm(count, 4, 1, lanes), vm(count, 4, 1, lanes),
        ]

    fine, mid, low = (16, 96, 256), (8, 48, 128), (4, 24, 64)
    scratch = [
        vm(*fine), vm(*fine), vm(*fine), vm(*fine), vm(*fine), vm(*fine),
        vm(*mid), vm(*mid), vm(*mid), vm(*mid), vm(*mid),
        vm(*low), vm(*low), vm(*low), vm(*low),
        vm(8, 256, 256, dtype=BF), vm(4, 256, 256, dtype=BF),
        vm(2, 256, 256, dtype=BF), vm(1, 64, 256, dtype=BF),
        vm(1, 256, 512, dtype=BF), vm(1, 256, 192, dtype=BF),
        vm(4, 256, 256, dtype=BF), vm(4, 128, 128, dtype=BF),
        vm(1, 256, 128, dtype=BF), vm(1, 32, 128, dtype=BF),
        vm(2, 2, 64, 64, dtype=BF), vm(2, 2, 48, 48, dtype=BF),
        vm(1, 2, 64, 256, dtype=BF), vm(1, 256, 48, dtype=BF),
        vm(1536, 3072), vm(64, 768, dtype=BF), vm(768, 128, dtype=BF), vm(128, 768, dtype=BF),
        vm(16, 768), vm(128, 3072, dtype=BF), vm(8, 3072), vm(1536, 128),
        vm(64, 128), vm(64, 1, 128), vm(devices, 1, 128),
        vm(devices, 128), vm(devices, 1, 128), vm(devices, 1, 128),
        vm(24, 64), vm(2, 1, 64), vm(24, 64), vm(3, 1, 64),
        vm(16, 256), vm(16, 128), vm(16, 64),
        *face_buffers(4, *fine), *face_buffers(3, *mid), *face_buffers(2, *low),
        pltpu.SemaphoreType.DMA((10, 8)), pltpu.SemaphoreType.DMA((10, 8)),
        pltpu.SemaphoreType.DMA((2,)), pltpu.SemaphoreType.DMA((4,)),
        pltpu.SemaphoreType.REGULAR, pltpu.SemaphoreType.DMA((2,)),
    ]
    in_vmem = pl.BlockSpec(memory_space=pltpu.VMEM)
    in_smem = pl.BlockSpec(memory_space=pltpu.SMEM)
    anywhere = pl.BlockSpec(memory_space=pl.ANY)
    call = pl.pallas_call(
        functools.partial(
            kernel, n_axial=lax.axis_size("axial"), n_azim=lax.axis_size("azim")
        ),
        out_shape=jax.ShapeDtypeStruct(residual.shape, F32),
        in_specs=[anywhere, in_vmem, in_vmem, anywhere] + [in_smem] * 10,
        out_specs=anywhere,
        scratch_shapes=scratch,
        compiler_params=pltpu.CompilerParams(
            collective_id=0, has_side_effects=True, vmem_limit_bytes=58 * 1024 * 1024
        ),
        cost_estimate=pl.CostEstimate(
            flops=12_000_000_000, bytes_accessed=24_000_000, transcendentals=0
        ),
    )
    return call(
        residual, jnp.transpose(element_scale, (0, 2, 1, 3)), vertex_route.reshape(1, -1), coarse_inverse,
        basis_fine, eigen_fine, operator_fine, basis_mid, eigen_mid, operator_mid,
        basis_low, eigen_low, prolong_mid.T, prolong_low.T,
    )


def solution(mesh):
    return jax.shard_map(
        on_device,
        mesh=mesh,
        in_specs=(
            P("axial", "azim", None),
            P(None, "axial", "azim", None),
            P(), P(), P(), P(), P(), P(), P(), P(), P(), P(),
            P("axial", "azim", None, None),
            P("axial", "azim", None, None),
        ),
        out_specs=P("axial", "azim", None),
        check_vma=False,
    )
```
